256 devices in a mesh: doc: 32 (over z, x), head: 8 (over y, core).
Axes of the slice: x: 4, y: 4, z: 8, core: 2. Of those that a mesh axis runs over, the one named last changes fastest.
Arguments:
- q_nope: bfloat16 [4096, 8192], P('doc', 'head'), may hold values from -6 to 6
- q_rope: bfloat16 [4096, 4096], P('doc', 'head'), may hold values from -8 to 8
- question_latent: bfloat16 [4096, 576], P('doc'), may hold values from -8 to 8
- doc_cache: bfloat16 [512, 512, 576], P('doc', 'head'), may hold values from -8 to 8
- w_uk: bfloat16 [64, 128, 512], P('head'), may hold values from -0.25 to 0.25
- w_uv: bfloat16 [64, 512, 128], P('head'), may hold values from -2 to 2
- doc_slot: int32 [512], replicated, may hold values from 0 to 511, as said below
- doc_blocks: int32 [512], replicated, may hold values from 1 to 4, 1280 in all
- pair_doc: int32 [1024], P('doc'), may hold values from 0 to 511, as said below
- pair_req: int32 [1024], P('doc'), may hold values from 0 to 7
Outputs:
- attn_values: bfloat16 [4096, 8192], P('doc', 'head')
The draws below stay inside these ranges and needn't reach their ends.
Inputs may be any that keep to these rules, and one draw needn't show every extreme that they name: doc_slot is a permutation: every row of doc_cache holds exactly one document. `pair_doc`: pair k belongs to the index k // 32 of doc; no request names a document twice; the 32 pairs of one index of doc name at most 2 documents stored on any one index of doc, and in every draw some index of doc receives exactly 2 pairs from every index.
All inputs are finite; a program needn't handle non-finite values.
Results may differ from the reference program's by a relative error of at most 0.0065.
Values may be sent and summed in bfloat16 or wider, within the bound.
A program may use at most 256 MiB of HBM per device.

```python
import math
import jax
import jax.numpy as jnp
import numpy as np
from jax import lax

HEADS = 64
RANK = 512
ROPE = 64
NOPE = 128
VDIM = 128
Q_LEN = 16
REQ_DEV = 8
DOC_DEV = 16
DOC_LEN = 512
BLOCK = 128
LATENT = 576
NBLK = 4
PAIRS = 32
CAP = 2
DOCS = 512
REQUESTS = 256
TOKENS = 4096
PAIRS_ALL = 1024
N_DOC = 32


def routing(key):
    key_place, key_popular, key_selection, key_combo = jax.random.split(jax.random.fold_in(key, 202), 4)
    doc_slot = jax.random.permutation(key_place, jnp.arange(DOCS, dtype=jnp.int32))
    lottery_entries = N_DOC * CAP
    popular = jax.random.permutation(key_popular, jnp.arange(N_DOC, dtype=jnp.int32))
    destination = jnp.arange(lottery_entries, dtype=jnp.int32) // CAP
    demand_level = popular[destination]
    frequent_reward = jnp.where(demand_level == N_DOC - 1, 4 * N_DOC, 0).astype(jnp.int32)
    lottery_score = jax.random.randint(key_selection, (N_DOC, lottery_entries), 0, N_DOC, dtype=jnp.int32) + demand_level[None, :] + frequent_reward[None, :]
    lottery_score = lottery_score * lottery_entries + jnp.arange(lottery_entries, dtype=jnp.int32)[None, :]
    chosen = lax.top_k(lottery_score, PAIRS)[1].astype(jnp.int32)
    combos = DOC_DEV * REQ_DEV
    shuffle_keys = jax.random.randint(key_combo, (N_DOC, N_DOC, combos), 0, 1 << 16, dtype=jnp.int32) * combos + jnp.arange(combos, dtype=jnp.int32)[None, None, :]
    shuffled = jnp.argsort(shuffle_keys, axis=2).astype(jnp.int32)
    chosen_dest = chosen // CAP
    selected_replica = chosen % CAP
    sources = jnp.broadcast_to(jnp.arange(N_DOC, dtype=jnp.int32)[:, None], (N_DOC, PAIRS))
    combination = shuffled[sources, chosen_dest, selected_replica]
    local_doc = combination % DOC_DEV
    request = combination // DOC_DEV
    slot_index = chosen_dest * DOC_DEV + local_doc
    inverse = jnp.argsort(doc_slot).astype(jnp.int32)
    document = inverse[slot_index]
    return (doc_slot, document.reshape(-1).astype(jnp.int32), request.reshape(-1).astype(jnp.int32))


def draw_doc_slot(key, part):
    shared = routing(key)
    return shared[0]


def draw_pair_doc(key, part):
    shared = routing(key)
    return shared[1]


def draw_pair_req(key, part):
    shared = routing(key)
    return shared[2]


def draw_q_rope(key, part):
    key = jax.random.fold_in(key, 4)
    base_key = jax.random.fold_in(key, 0)
    drawn = jnp.clip(jax.random.normal(base_key, (TOKENS, HEADS, ROPE), jnp.float32), -6.0, 6.0)
    return drawn.reshape(TOKENS, HEADS * ROPE).astype(jnp.bfloat16)


def draw_question_latent(key, part):
    key = jax.random.fold_in(key, 5)
    drawn = jnp.clip(jax.random.normal(key, (TOKENS, LATENT), jnp.float32), -6.0, 6.0)
    return drawn.astype(jnp.bfloat16)


def draw_doc_cache(key, part):
    key = jax.random.fold_in(key, 6)
    drawn = jnp.clip(jax.random.normal(key, (DOCS, DOC_LEN, LATENT), jnp.float32), -6.0, 6.0)
    return drawn.astype(jnp.bfloat16)


def block_scale(key, shape, cuts, low, high):
    factor_of = 1.0
    for dim, blocks in cuts:
        draws = jax.random.uniform(jax.random.fold_in(jax.random.fold_in(key, 6), dim), (blocks,), jnp.float32, low / len(cuts), high / len(cuts))
        factor_of = factor_of * jnp.repeat(jnp.exp(draws), shape[dim] // blocks).reshape((-1,) + (1,) * (len(shape) - 1 - dim))
    return factor_of


def profile(count, total, reach, skew):
    loads = [(1 << 20) // math.isqrt(rank ** skew) + 1 for rank in range(2, count + 1)]
    rest, given = total - reach - (count - 1), [1] * (count - 1)
    while rest > 0:
        free = [i for i in range(count - 1) if given[i] < reach]
        pool, left = sum([loads[i] for i in free]), rest
        for i in free:
            addition = min(reach - given[i], max(1, left * loads[i] // pool), rest)
            given[i] = given[i] + addition
            rest = rest - addition
    return np.array([reach] + given)


def uneven(key, count, total, reach, slope):
    if count == 2:
        one = jax.random.randint(key, (), max(1, total - reach), min(reach, total - 1) + 1)
        return jnp.stack([one, total - one])
    lengths = jnp.asarray(profile(count, total, reach, slope), jnp.int32)
    twos = (count - 1) // 2
    donor, sink = lengths[1:1 + 2 * twos:2], lengths[2:2 + 2 * twos:2]
    margin = jnp.minimum(donor - 1, reach - sink)
    shifted = jax.random.randint(jax.random.fold_in(key, 1), (twos,), 0, 1 << 20) % (margin + 1)
    lengths = lengths.at[1:1 + 2 * twos:2].set(donor - shifted).at[2:2 + 2 * twos:2].set(sink + shifted)
    return lengths[jax.random.permutation(jax.random.fold_in(key, 2), count)]


def gaussian(rng, dims, width, bound, pieces=(), held_as=jnp.bfloat16):
    loudness = block_scale(rng, dims, pieces, -0.22, 0.18) if pieces else 1.0
    values = jax.random.normal(rng, dims, jnp.float32) * width * loudness
    return jnp.minimum(jnp.maximum(values, -bound), bound).astype(held_as)


def setup_inputs(seed: int = 0) -> dict:
    key_of = jax.random.split(jax.random.key(seed), 11)
    q_nope = gaussian(key_of[0], (TOKENS, HEADS * NOPE), 1.0, 6.0, ((0, 32), (1, 8)))
    q_rope = draw_q_rope(jax.random.fold_in(key_of[10], 71), 0)
    question_latent = draw_question_latent(jax.random.fold_in(key_of[10], 71), 0)
    doc_cache = draw_doc_cache(jax.random.fold_in(key_of[10], 71), 0)
    w_uk = gaussian(key_of[4], (HEADS, NOPE, RANK), RANK ** -0.5, 0.25, ((0, 8),))
    w_uv = gaussian(key_of[5], (HEADS, RANK, VDIM), (max(1, RANK // 64)) ** -0.5, 2.0, ((0, 8),))
    doc_slot = draw_doc_slot(jax.random.fold_in(key_of[10], 71), 0)
    doc_blocks = uneven(key_of[7], DOCS, DOCS * (NBLK + 1) // 2, NBLK, 1).astype(jnp.int32)
    pair_doc = draw_pair_doc(jax.random.fold_in(key_of[10], 71), 0)
    pair_req = draw_pair_req(jax.random.fold_in(key_of[10], 71), 0)
    return {"q_nope": q_nope, "q_rope": q_rope, "question_latent": question_latent, "doc_cache": doc_cache, "w_uk": w_uk, "w_uv": w_uv, "doc_slot": doc_slot, "doc_blocks": doc_blocks, "pair_doc": pair_doc, "pair_req": pair_req}


LOWEST = -1.0e30


def partial_terms(query_rows, key_rows, visible, w_uv):
    score_scale = (NOPE + ROPE) ** -0.5
    scores = jnp.einsum("qhc,kc->qhk", query_rows.astype(jnp.float32), key_rows.astype(jnp.float32)) * score_scale
    key_mask = visible[:, None, :]
    scores = jnp.where(key_mask, scores, LOWEST)
    maxima = jnp.max(scores, axis=2)
    weights = jnp.where(key_mask, jnp.exp(scores - maxima[:, :, None]), 0.0)
    totals = jnp.sum(weights, axis=2)
    probabilities = weights.astype(jnp.bfloat16)
    latent = jnp.einsum("qhk,kc->qhc", probabilities.astype(jnp.float32), key_rows[:, :RANK].astype(jnp.float32)).astype(jnp.bfloat16)
    projected = jnp.einsum("qhc,hcd->qhd", latent.astype(jnp.float32), w_uv.astype(jnp.float32))
    normed = (projected / totals[:, :, None]).astype(jnp.bfloat16)
    return maxima, totals, normed


def reference(q_nope, q_rope, question_latent, doc_cache, w_uk, w_uv, doc_slot, doc_blocks, pair_doc, pair_req):
    uk_float = w_uk.astype(jnp.float32)

    def absorb(rows):
        nope_rows, rope_rows = rows
        absorbed = jnp.einsum("thn,hnc->thc", nope_rows.reshape(Q_LEN, HEADS, NOPE).astype(jnp.float32), uk_float).astype(jnp.bfloat16)
        return jnp.concatenate([absorbed, rope_rows.reshape(Q_LEN, HEADS, ROPE)], axis=2)

    queries = lax.map(absorb, (q_nope.reshape(REQUESTS, Q_LEN, HEADS * NOPE), q_rope.reshape(REQUESTS, Q_LEN, HEADS * ROPE)))
    own_keys = question_latent.reshape(REQUESTS, Q_LEN, RANK + ROPE)
    places = jnp.arange(Q_LEN, dtype=jnp.int32)
    causal = places[None, :] <= places[:, None]

    def own_term(rows):
        maxima, totals, normed = partial_terms(rows[0], rows[1], causal, w_uv)
        return maxima, totals, totals[:, :, None] * normed.astype(jnp.float32)

    maxima, totals, weighted = lax.map(own_term, (queries, own_keys))
    key_places = jnp.arange(DOC_LEN, dtype=jnp.int32)

    def visit(carried, pair_data):
        maxima, totals, weighted = carried
        pair_index, document, local_request = pair_data
        request = (pair_index // PAIRS) * REQ_DEV + local_request
        slot_index = lax.dynamic_index_in_dim(doc_slot, document, 0, keepdims=False)
        blocks = lax.dynamic_index_in_dim(doc_blocks, document, 0, keepdims=False)
        key_rows = lax.dynamic_index_in_dim(doc_cache, slot_index, 0, keepdims=False)
        visible = jnp.broadcast_to(key_places[None, :] < blocks * BLOCK, (Q_LEN, DOC_LEN))
        query_rows = lax.dynamic_index_in_dim(queries, request, 0, keepdims=False)
        pair_max, pair_total, normed = partial_terms(query_rows, key_rows, visible, w_uv)
        old_max = lax.dynamic_index_in_dim(maxima, request, 0, keepdims=False)
        old_total = lax.dynamic_index_in_dim(totals, request, 0, keepdims=False)
        old_sum = lax.dynamic_index_in_dim(weighted, request, 0, keepdims=False)
        largest = jnp.maximum(old_max, pair_max)
        retained = jnp.exp(old_max - largest)
        fresh_weight = jnp.exp(pair_max - largest) * pair_total
        updated_total = retained * old_total + fresh_weight
        new_sum = retained[:, :, None] * old_sum + fresh_weight[:, :, None] * normed.astype(jnp.float32)
        maxima = lax.dynamic_update_index_in_dim(maxima, largest, request, 0)
        totals = lax.dynamic_update_index_in_dim(totals, updated_total, request, 0)
        weighted = lax.dynamic_update_index_in_dim(weighted, new_sum, request, 0)
        return (maxima, totals, weighted), None

    indices = jnp.arange(PAIRS_ALL, dtype=jnp.int32)
    (maxima, totals, weighted), _ = lax.scan(visit, (maxima, totals, weighted), (indices, pair_doc, pair_req))
    result = (weighted / totals[..., None]).astype(jnp.bfloat16)
    return result.reshape(TOKENS, HEADS * VDIM)
```

```python
import functools

import jax
import jax.numpy as jnp
from jax import lax
from jax.experimental import pallas as pl
from jax.experimental.pallas import tpu as pltpu
from jax.sharding import PartitionSpec as P

RANK = 512
ROPE = 64
NOPE = 128
VDIM = 128
LATENT = RANK + ROPE
Q_LEN = 16
BLOCK = 128
NBLK = 4
HD = 8
TOK = 128
REQ = 8
DOC_DEV = 16
PAIRS = 32
CAP = 2
ROWS = CAP * Q_LEN
NX, NZ, NY = 4, 8, 4
N_DOC = NX * NZ
SLOTS = N_DOC * CAP
QW = HD * (NOPE + ROPE)
VW = HD * VDIM
POS = 64
SCALE = (NOPE + ROPE) ** (-0.5)
LOWEST = -1e30
MESH = pl.DeviceIdType.MESH
F32 = jnp.float32
BF16 = jnp.bfloat16
VMEM_LIMIT = 56 * 1024 * 1024


def dot(a, b, dims):
    return lax.dot_general(a, b, (dims, ((), ())), preferred_element_type=F32)


def greet(peers):
    barrier = pltpu.get_barrier_semaphore()
    for peer in peers:
        pl.semaphore_signal(barrier, inc=1, device_id=peer, device_id_type=MESH)
    pl.semaphore_wait(barrier, len(peers))


def spread_kernel(
    q_ref, tbl_ref, doc_ref, slots_ref, tblout_ref, full_ref,
    gq, sendb, tblb, zs, zr, ts, tr, us, ur, xs, xr, ys, yr, cs, cr, ls,
):
    d = lax.axis_index("doc")
    h = lax.axis_index("head")
    z, x = d // NX, d % NX
    y, c = h // 2, h % 2
    right = (((z + 1) % NZ) * NX + x, h)
    left = (((z + NZ - 1) % NZ) * NX + x, h)
    z_peer = [None] + [(((z + j) % NZ) * NX + x, h) for j in range(1, NZ)]
    x_peer = [None] + [(z * NX + (x + j) % NX, h) for j in range(1, NX)]
    h_up = ((y + 1) % NY) * 2 + c
    h_down = ((y + NY - 1) % NY) * 2 + c
    h_far = ((y + 2) % NY) * 2 + c
    up, down, other = (d, h_up), (d, h_down), (d, y * 2 + 1 - c)
    greet(z_peer[1:] + x_peer[1:] + [up, down, other])

    def remote(src, dst, send, recv, peer):
        return pltpu.make_async_remote_copy(
            src_ref=src, dst_ref=dst, send_sem=send, recv_sem=recv, device_id=peer, device_id_type=MESH
        )

    def ring(i, src, dst, peer):
        return remote(src, dst, zs.at[i], zr.at[i], peer)

    half = TOK // 2
    low, high = pl.ds(0, half), pl.ds(half, half)
    ring_copies = [
        ring(0, q_ref, gq.at[7], right),
        ring(1, q_ref, gq.at[1], left),
        ring(2, gq.at[7], gq.at[6], right),
        ring(3, gq.at[1], gq.at[2], left),
        ring(4, gq.at[6], gq.at[5], right),
        ring(5, gq.at[2], gq.at[3], left),
        ring(6, gq.at[5, low], gq.at[4, low], right),
        ring(7, gq.at[3, high], gq.at[4, high], left),
    ]
    ring_copies[0].start()
    ring_copies[1].start()

    tables = [
        remote(tbl_ref.at[(z + j) % NZ], tblb.at[z], ts.at[j], tr.at[j], z_peer[j]) for j in range(1, NZ)
    ]
    for copy in tables:
        copy.start()

    def place(head):
        return full_ref.at[:, pl.ds(pl.multiple_of(head * POS, POS), POS), :]

    def part(head, first):
        return full_ref.at[
            pl.ds(first, DOC_DEV // 2), pl.ds(pl.multiple_of(head * POS, POS), POS), :
        ]

    own_docs = pltpu.make_async_copy(doc_ref, place(h), ls.at[0])
    docs_up = remote(doc_ref, place(h), ys.at[0], yr.at[0], up)
    docs_down = remote(doc_ref, place(h), ys.at[1], yr.at[1], down)
    docs_other = remote(doc_ref, place(h), cs.at[0], cr.at[0], other)
    docs_up.start()
    docs_down.start()
    docs_other.start()
    own_docs.start()

    tblb[pl.ds(z, 1)] = tbl_ref[pl.ds(z, 1)]
    for copy in tables:
        copy.wait_recv()
    passed = [
        remote(tblb, tblout_ref.at[x], us.at[j], ur.at[j], x_peer[j]) for j in range(1, NX)
    ]
    for copy in passed:
        copy.start()
    own_table = pltpu.make_async_copy(tblb, tblout_ref.at[x], ls.at[1])
    own_table.start()

    token = lax.broadcasted_iota(jnp.int32, (TOK, NX * ROWS), 0)
    pending = []

    def forward(rel):
        owner = (z + rel) % NZ
        wanted = tblb[owner][:, 0:TOK]
        pick = jnp.where(token == wanted, 1.0, 0.0).astype(BF16)
        source = q_ref if rel == 0 else gq.at[rel]
        for k in range(0, QW, 512):
            chosen = dot(pick, source[:, k : k + 512], ((0,), (0,))).astype(BF16)
            sendb[rel, :, :, k : k + 512] = chosen.reshape(NX, ROWS, 512)
        target = slots_ref.at[owner * NX + x]
        for j in range(1, NX):
            copy = remote(
                sendb.at[rel, (x + j) % NX], target, xs.at[rel, j], xr.at[rel, j], x_peer[j]
            )
            copy.start()
            pending.append(copy)
        copy = pltpu.make_async_copy(sendb.at[rel, x], target, ls.at[2 + rel])
        copy.start()
        kept.append(copy)

    kept = [own_docs, own_table]
    forward(0)
    for i, (a, b) in enumerate(((7, 1), (6, 2), (5, 3))):
        ring_copies[2 * i].wait_recv()
        ring_copies[2 * i + 2].start()
        ring_copies[2 * i + 1].wait_recv()
        ring_copies[2 * i + 3].start()
        forward(a)
        forward(b)

    docs_up.wait_recv()
    pass_up = remote(part(h_down, 0), part(h_down, 0), ys.at[2], yr.at[2], up)
    pass_up.start()
    cross_down = remote(place(h_down), place(h_down), cs.at[1], cr.at[1], other)
    cross_down.start()
    docs_down.wait_recv()
    pass_down = remote(part(h_up, 8), part(h_up, 8), ys.at[3], yr.at[3], down)
    pass_down.start()
    cross_up = remote(place(h_up), place(h_up), cs.at[2], cr.at[2], other)
    cross_up.start()

    ring_copies[6].wait_recv()
    ring_copies[7].wait_recv()
    forward(4)

    pass_up.wait_recv()
    pass_down.wait_recv()
    cross_far = remote(place(h_far), place(h_far), cs.at[3], cr.at[3], other)
    cross_far.start()

    for copy in pending + passed + [docs_other, cross_down, cross_up, cross_far]:
        copy.wait_recv()
    for copy in kept:
        copy.wait()
    for copy in (
        ring_copies + tables + passed + pending
        + [docs_up, docs_down, docs_other, pass_up, pass_down, cross_down, cross_up, cross_far]
    ):
        copy.wait_send()


def spread(q, table, doc_cache):
    anywhere = pl.BlockSpec(memory_space=pl.ANY)
    local = pl.BlockSpec(memory_space=pltpu.VMEM)
    dma = pltpu.SemaphoreType.DMA
    return pl.pallas_call(
        spread_kernel,
        out_shape=(
            jax.ShapeDtypeStruct((N_DOC, ROWS, QW), BF16),
            jax.ShapeDtypeStruct((NX, NZ, 1, 256), jnp.int32),
            jax.ShapeDtypeStruct((DOC_DEV, NBLK * BLOCK, LATENT), BF16),
        ),
        in_specs=[local, local, anywhere],
        out_specs=(anywhere, anywhere, anywhere),
        scratch_shapes=[
            pltpu.VMEM((NZ, TOK, QW), BF16),
            pltpu.VMEM((NZ, NX, ROWS, QW), BF16),
            pltpu.VMEM((NZ, 1, 256), jnp.int32),
            dma((8,)), dma((8,)),
            dma((NZ,)), dma((NZ,)),
            dma((NX,)), dma((NX,)),
            dma((NZ, NX)), dma((NZ, NX)),
            dma((4,)), dma((4,)),
            dma((4,)), dma((4,)),
            dma((10,)),
        ],
        compiler_params=pltpu.CompilerParams(
            collective_id=0, has_side_effects=True, vmem_limit_bytes=VMEM_LIMIT
        ),
        name="spread",
    )(q, table, doc_cache)


def softmax_rows(scores):
    largest = jnp.max(scores, axis=1, keepdims=True)
    weights = jnp.exp((scores - largest) * SCALE)
    totals = jnp.sum(weights, axis=1, keepdims=True)
    return weights.astype(BF16), totals, largest * SCALE + jnp.log(totals)


def attend_kernel(
    code_ref, blk_ref, slots_ref, full_ref, uk_ref, uv_ref, out_ref, lse_ref, qa, qr
):
    for head in range(HD):
        nope = slots_ref[:, :, head * NOPE : (head + 1) * NOPE].reshape(SLOTS * Q_LEN, NOPE)
        absorbed = dot(nope, uk_ref[head], ((1,), (0,))).astype(BF16)
        qa[:, head] = absorbed.reshape(SLOTS, Q_LEN, RANK)
        first = HD * NOPE + head * ROPE
        rope = slots_ref[:, :, first : first + ROPE].reshape(SLOTS, Q_LEN, ROPE)
        qr[:, head] = rope

    row = lax.broadcasted_iota(jnp.int32, (TOK, TOK), 0)
    column = lax.broadcasted_iota(jnp.int32, (TOK, TOK), 1)
    diagonal = row == column

    def one_slot(s, carry):
        blocks = blk_ref[s]
        doc = code_ref[s]
        for count in range(1, NBLK + 1):

            @pl.when(blocks == count)
            def _():
                length = count * BLOCK
                latent_q = qa[s].reshape(HD * Q_LEN, RANK)
                rope_q = qr[s].reshape(HD * Q_LEN, ROPE)
                keys = full_ref[doc, 0:length, 0:RANK]
                rope_k = full_ref[doc, 0:length, RANK:LATENT]
                scores = dot(latent_q, keys, ((1,), (1,))) + dot(rope_q, rope_k, ((1,), (1,)))
                weights, totals, lse = softmax_rows(scores)
                latent = dot(weights, keys, ((1,), (0,))) / totals
                qa[s] = latent.astype(BF16).reshape(HD, Q_LEN, RANK)
                lse_ref[s] = jnp.sum(jnp.where(diagonal, lse, 0.0), axis=0, keepdims=True)

        return carry

    lax.fori_loop(0, SLOTS, one_slot, 0)

    for head in range(HD):
        latent = qa[:, head].reshape(SLOTS * Q_LEN, RANK)
        values = dot(latent, uv_ref[head], ((1,), (0,))).astype(BF16)
        out_ref[:, :, head * VDIM : (head + 1) * VDIM] = values.reshape(N_DOC, ROWS, VDIM)


def attend(code, blocks, slots, full_cache, w_uk, w_uv):
    smem = pl.BlockSpec(memory_space=pltpu.SMEM)
    local = pl.BlockSpec(memory_space=pltpu.VMEM)
    return pl.pallas_call(
        attend_kernel,
        out_shape=(
            jax.ShapeDtypeStruct((N_DOC, ROWS, VW), BF16),
            jax.ShapeDtypeStruct((SLOTS, 1, TOK), F32),
        ),
        in_specs=[smem, smem, local, local, local, local],
        out_specs=(local, local),
        scratch_shapes=[
            pltpu.VMEM((SLOTS, HD, Q_LEN, RANK), BF16),
            pltpu.VMEM((SLOTS, HD, Q_LEN, ROPE), BF16),
        ],
        compiler_params=pltpu.CompilerParams(vmem_limit_bytes=VMEM_LIMIT),
        name="attend",
    )(code, blocks, slots, full_cache, w_uk, w_uv)


def give_back_kernel(val_ref, lse_ref, val_out, lse_out, vs, vr, es, er, ls):
    d = lax.axis_index("doc")
    h = lax.axis_index("head")
    barrier = pltpu.get_barrier_semaphore()

    def hello(j, carry):
        pl.semaphore_signal(barrier, inc=1, device_id=((d + j) % N_DOC, h), device_id_type=MESH)
        return carry

    lax.fori_loop(1, N_DOC, hello, 0)
    pl.semaphore_wait(barrier, N_DOC - 1)

    def copies(j):
        peer = (d + j) % N_DOC
        return [
            pltpu.make_async_remote_copy(
                src_ref=src.at[peer], dst_ref=dst.at[d], send_sem=send.at[j], recv_sem=recv.at[j],
                device_id=(peer, h), device_id_type=MESH,
            )
            for src, dst, send, recv in ((val_ref, val_out, vs, vr), (lse_ref, lse_out, es, er))
        ]

    def begin(j, carry):
        for copy in copies(j):
            copy.start()
        return carry

    def end(j, carry):
        for copy in copies(j):
            copy.wait()
        return carry

    lax.fori_loop(1, N_DOC, begin, 0)
    kept = [
        pltpu.make_async_copy(val_ref.at[d], val_out.at[d], ls.at[0]),
        pltpu.make_async_copy(lse_ref.at[d], lse_out.at[d], ls.at[1]),
    ]
    for copy in kept:
        copy.start()
    lax.fori_loop(1, N_DOC, end, 0)
    for copy in kept:
        copy.wait()


def give_back(values, lse):
    anywhere = pl.BlockSpec(memory_space=pl.ANY)
    dma = pltpu.SemaphoreType.DMA
    return pl.pallas_call(
        give_back_kernel,
        out_shape=(
            jax.ShapeDtypeStruct(values.shape, BF16),
            jax.ShapeDtypeStruct(lse.shape, F32),
        ),
        in_specs=[anywhere, anywhere],
        out_specs=(anywhere, anywhere),
        scratch_shapes=[dma((N_DOC,)), dma((N_DOC,)), dma((N_DOC,)), dma((N_DOC,)), dma((2,))],
        compiler_params=pltpu.CompilerParams(collective_id=1, has_side_effects=True),
        name="give_back",
    )(values, lse)


def merge_kernel(
    pos_ref, req_ref, q_ref, ql_ref, uk_ref, uv_ref, val_ref, lse_ref, out_ref, top, den, acc
):
    row = lax.broadcasted_iota(jnp.int32, (TOK, TOK), 0)
    column = lax.broadcasted_iota(jnp.int32, (TOK, TOK), 1)
    visible = (row // Q_LEN == column // Q_LEN) & (column <= row)
    diagonal = row == column
    keys = ql_ref[:, 0:RANK]
    rope_k = ql_ref[:, RANK:LATENT]
    for head in range(HD):
        nope = q_ref[:, head * NOPE : (head + 1) * NOPE]
        first = HD * NOPE + head * ROPE
        absorbed = dot(nope, uk_ref[head], ((1,), (0,))).astype(BF16)
        scores = dot(absorbed, keys, ((1,), (1,))) + dot(
            q_ref[:, first : first + ROPE], rope_k, ((1,), (1,))
        )
        weights, totals, lse = softmax_rows(jnp.where(visible, scores, LOWEST))
        latent = (dot(weights, keys, ((1,), (0,))) / totals).astype(BF16)
        values = dot(latent, uv_ref[head], ((1,), (0,))).astype(BF16).astype(F32)
        acc[:, head] = values.reshape(REQ, Q_LEN, VDIM)
        top[:, head] = jnp.broadcast_to(lse, (TOK, VDIM)).reshape(REQ, Q_LEN, VDIM)
    den[...] = jnp.ones_like(den)

    def one_pair(k, carry):
        slot = pos_ref[k]
        request = req_ref[k]
        lse = jnp.sum(jnp.where(diagonal, lse_ref[slot], 0.0), axis=1, keepdims=True)
        lse = jnp.broadcast_to(lse, (TOK, VDIM)).reshape(HD, Q_LEN, VDIM)
        values = val_ref[slot]
        for head in range(HD):
            old = top[request, head]
            new = jnp.maximum(old, lse[head])
            keep = jnp.exp(old - new)
            fresh = jnp.exp(lse[head] - new)
            part = values[:, head * VDIM : (head + 1) * VDIM].astype(F32)
            top[request, head] = new
            den[request, head] = den[request, head] * keep + fresh
            acc[request, head] = acc[request, head] * keep + fresh * part
        return carry

    lax.fori_loop(0, PAIRS, one_pair, 0)
    for head in range(HD):
        result = (acc[:, head] / den[:, head]).astype(BF16)
        out_ref[:, head * VDIM : (head + 1) * VDIM] = result.reshape(TOK, VDIM)


def merge(position, request, q, question_latent, w_uk, w_uv, values, lse):
    smem = pl.BlockSpec(memory_space=pltpu.SMEM)
    local = pl.BlockSpec(memory_space=pltpu.VMEM)
    return pl.pallas_call(
        merge_kernel,
        out_shape=jax.ShapeDtypeStruct((TOK, VW), BF16),
        in_specs=[smem, smem] + [local] * 6,
        out_specs=local,
        scratch_shapes=[pltpu.VMEM((REQ, HD, Q_LEN, VDIM), F32)] * 3,
        compiler_params=pltpu.CompilerParams(vmem_limit_bytes=VMEM_LIMIT),
        name="merge",
    )(position, request, q, question_latent, w_uk, w_uv, values, lse)


def on_device(
    q_nope, q_rope, question_latent, doc_cache, w_uk, w_uv, doc_slot, doc_blocks, pair_doc, pair_req
):
    device = lax.axis_index("doc")
    q = jnp.concatenate([q_nope, q_rope], axis=1)
    doc_ids = jnp.arange(doc_slot.shape[0], dtype=jnp.int32)
    matches = pair_doc[:, None] == doc_ids[None, :]
    pair_slot = jnp.sum(jnp.where(matches, doc_slot[None, :], 0), axis=1)
    target = pair_slot // DOC_DEV
    sequence = jnp.arange(PAIRS, dtype=jnp.int32)
    before = (target[:, None] == target[None, :]) & (sequence[None, :] < sequence[:, None])
    position = target * CAP + jnp.sum(before.astype(jnp.int32), axis=1)
    placed = jnp.arange(SLOTS, dtype=jnp.int32)[:, None] == position[None, :]
    first_token = jnp.sum(jnp.where(placed, pair_req[None, :] * Q_LEN + 1, 0), axis=1) - 1
    code = jnp.sum(jnp.where(placed, pair_slot[None, :] % DOC_DEV + 1, 0), axis=1)
    tokens = jnp.where(
        first_token[:, None] >= 0, first_token[:, None] + jnp.arange(Q_LEN, dtype=jnp.int32), -1
    )
    table = jnp.concatenate(
        [
            tokens.reshape(NZ, 1, NX * ROWS),
            jnp.broadcast_to(code[:, None], (SLOTS, Q_LEN)).reshape(NZ, 1, NX * ROWS),
        ],
        axis=2,
    )
    owned = doc_slot[None, :] == device * DOC_DEV + jnp.arange(DOC_DEV, dtype=jnp.int32)[:, None]
    owned_blocks = jnp.sum(jnp.where(owned, doc_blocks[None, :], 0), axis=1)

    slots, tables, full_cache = spread(q, table, doc_cache)

    got = tables.reshape(NX, NZ, 2, NX, CAP, Q_LEN)[:, :, 1, :, :, 0]
    mine = jnp.arange(NX, dtype=jnp.int32) == device % NX
    got = jnp.sum(jnp.where(mine[None, None, :, None], got, 0), axis=2)
    got = got.transpose(1, 0, 2).reshape(SLOTS)
    chooser = got[:, None] == jnp.arange(1, DOC_DEV + 1, dtype=jnp.int32)[None, :]
    blocks = jnp.sum(jnp.where(chooser, owned_blocks[None, :], 0), axis=1)
    values, lse = attend(jnp.maximum(got - 1, 0), blocks, slots, full_cache, w_uk, w_uv)
    values, lse = give_back(values, lse.reshape(N_DOC, CAP, TOK))
    return merge(
        position, pair_req, q, question_latent, w_uk, w_uv,
        values.reshape(SLOTS, Q_LEN, VW), lse.reshape(SLOTS, 1, TOK),
    )


def solution(mesh):
    placed = (
        P("doc", "head"),
        P("doc", "head"),
        P("doc", None),
        P("doc", "head", None),
        P("head", None, None),
        P("head", None, None),
        P(),
        P(),
        P("doc"),
        P("doc"),
    )
    return jax.shard_map(
        on_device, mesh=mesh, in_specs=placed, out_specs=P("doc", "head"), check_vma=False
    )
```

```python
import jax
import jax.numpy as jnp
from jax import lax
from jax.experimental import pallas as pl
from jax.experimental.pallas import tpu as pltpu
from jax.sharding import PartitionSpec as P

RANK = 512
ROPE = 64
NOPE = 128
VDIM = 128
LATENT = RANK + ROPE
Q_LEN = 16
BLOCK = 128
DOC_LEN = 512
HD = 8
TOK = 128
REQ = 8
DOC_DEV = 16
PAIRS = 32
CAP = 2
ROWS = CAP * Q_LEN
NX, NZ, NY = 4, 8, 4
N_DOC = NX * NZ
SLOTS = N_DOC * CAP
GROUP = NX * CAP
OWN = NZ
NW = HD * NOPE
QW = HD * (NOPE + ROPE)
VW = HD * VDIM
POS = 64
TBL = 3 * NX * ROWS
SCALE = (NOPE + ROPE) ** (-0.5)
LN2 = 0.6931471805599453
EXP2_SCALE = SCALE / LN2
LOWEST = -1e30
MESH = pl.DeviceIdType.MESH
F32 = jnp.float32
BF16 = jnp.bfloat16
VMEM_LIMIT = 58 * 1024 * 1024


def dot(a, b, dims):
    return lax.dot_general(a, b, (dims, ((), ())), preferred_element_type=F32)


def whole_kernel(
    qn_ref, qr_ref, ql_ref, tbl_ref, doc_ref, uk_ref, uv_ref, out_ref,
    full, gq, sendb, slots, tblb, tblx, sm_own, sm_got, qa, qrope, inv, vals, lses,
    xv, xl, pv, plse, inv_v, in_l,
    zs, zr, ts, tr, us, ur, xs, xr, ys, yr, cs, cr, vs, vr, es, er, ps, pr, fs, fr, ls,
):
    d = lax.axis_index("doc")
    h = lax.axis_index("head")
    z, x = d // NX, d % NX
    y, c = h // 2, h % 2
    z_peer = [None] + [(((z + j) % NZ) * NX + x, h) for j in range(1, NZ)]
    x_peer = [None] + [(z * NX + (x + j) % NX, h) for j in range(1, NX)]
    right, left = z_peer[1], z_peer[NZ - 1]
    h_up = ((y + 1) % NY) * 2 + c
    h_down = ((y + NY - 1) % NY) * 2 + c
    h_far = ((y + 2) % NY) * 2 + c
    up, down, other = (d, h_up), (d, h_down), (d, y * 2 + 1 - c)

    barrier = pltpu.get_barrier_semaphore()
    greeted = z_peer[1:] + x_peer[1:] + [up, down, other]
    for peer in greeted:
        pl.semaphore_signal(barrier, inc=1, device_id=peer, device_id_type=MESH)
    gq[0, :, 0:NW] = qn_ref[...]
    gq[0, :, NW:QW] = qr_ref[...]
    tblb[pl.ds(z, 1)] = tbl_ref[pl.ds(z, 1)]
    pl.semaphore_wait(barrier, len(greeted))

    sent = []

    def remote(src, dst, send, recv, peer):
        copy = pltpu.make_async_remote_copy(
            src_ref=src, dst_ref=dst, send_sem=send, recv_sem=recv, device_id=peer, device_id_type=MESH
        )
        copy.start()
        sent.append(copy)
        return copy

    half = TOK // 2
    low, high = pl.ds(0, half), pl.ds(half, half)

    def ring(i, src, dst, peer):
        return remote(src, dst, zs.at[i], zr.at[i], peer)

    ring_a = ring(0, gq.at[0], gq.at[7], right)
    ring_b = ring(1, gq.at[0], gq.at[1], left)
    tables = [
        remote(tbl_ref.at[(z + j) % NZ], tblb.at[z], ts.at[j], tr.at[j], z_peer[j]) for j in range(1, NZ)
    ]

    def place(head):
        return full.at[:, pl.ds(pl.multiple_of(head * POS, POS), POS), :]

    def part(head, first):
        return full.at[pl.ds(first, DOC_DEV // 2), pl.ds(pl.multiple_of(head * POS, POS), POS), :]

    docs_up = remote(doc_ref, place(h), ys.at[0], yr.at[0], up)
    docs_down = remote(doc_ref, place(h), ys.at[1], yr.at[1], down)
    docs_other = remote(doc_ref, place(h), cs.at[0], cr.at[0], other)
    own_docs = pltpu.make_async_copy(doc_ref, place(h), ls.at[0])
    own_docs.start()

    for copy in tables:
        copy.wait_recv()
    passed = [remote(tblb, tblx.at[x], us.at[j], ur.at[j], x_peer[j]) for j in range(1, NX)]
    tblx[pl.ds(x, 1)] = tblb[...].reshape(1, NZ, 1, TBL)
    own_table = pltpu.make_async_copy(tblb, sm_own, ls.at[1])
    own_table.start()

    token = lax.broadcasted_iota(jnp.int32, (TOK, NX * ROWS), 0)
    arriving = {}

    def picked(rel):
        wanted = tblb[(z + rel) % NZ][:, 0:TOK]
        return jnp.where(token == wanted, 1.0, 0.0).astype(BF16)

    def forward(rel):
        pick = picked(rel)
        for k in range(0, QW, 512):
            chosen = dot(pick, gq[rel, :, k : k + 512], ((0,), (0,))).astype(BF16)
            sendb[rel, :, :, k : k + 512] = chosen.reshape(NX, ROWS, 512)
        arriving[rel] = [
            remote(
                sendb.at[rel, (x + j) % NX], slots.at[rel, x], xs.at[rel, j], xr.at[rel, j], x_peer[j]
            )
            for j in range(1, NX)
        ]
        slots[rel, pl.ds(x, 1)] = sendb[rel, pl.ds(x, 1)]

    def absorb(group, rows):
        span = pl.ds(group * GROUP, GROUP)
        for head in range(HD):
            nope = rows(head * NOPE, NOPE).reshape(TOK, NOPE)
            absorbed = dot(nope, uk_ref[head], ((1,), (0,))).astype(BF16)
            qa[span, head] = absorbed.reshape(GROUP, Q_LEN, RANK)
            qrope[span, head] = rows(NW + head * ROPE, ROPE).reshape(GROUP, Q_LEN, ROPE)

    def take_in(rel):
        for copy in arriving[rel]:
            copy.wait_recv()
        absorb(rel, lambda first, width: slots[rel, :, :, first : first + width])

    row = lax.broadcasted_iota(jnp.int32, (TOK, TOK), 0)
    column = lax.broadcasted_iota(jnp.int32, (TOK, TOK), 1)
    diagonal = row == column

    def softmax(scores):
        largest = jnp.max(scores, axis=1, keepdims=True) * EXP2_SCALE
        weights = jnp.exp2(scores * EXP2_SCALE - largest)
        totals = jnp.sum(weights, axis=1, keepdims=True)
        lse = largest * LN2 + jnp.log(totals)
        as_row = jnp.sum(jnp.where(diagonal, lse, 0.0), axis=0, keepdims=True)
        return weights.astype(BF16), 1.0 / totals, as_row

    def finish(slot, i, weights, scale, keys):
        latent = dot(weights, keys, ((1,), (0,)))
        qa[slot] = latent.astype(BF16).reshape(HD, Q_LEN, RANK)
        inv[i] = jnp.broadcast_to(scale, (TOK, VDIM)).reshape(HD, Q_LEN, VDIM)

    def project(group, store):
        for head in range(HD):
            latent = qa[pl.ds(group * GROUP, GROUP), head].reshape(TOK, RANK)
            values = dot(latent, uv_ref[head], ((1,), (0,))) * inv[:, head].reshape(TOK, VDIM)
            store(head * VDIM, values.astype(BF16))

    def own_term():
        absorb(OWN, lambda first, width: gq[0, :, first : first + width])
        key_at = lax.broadcasted_iota(jnp.int32, (TOK, Q_LEN), 1)
        query_at = lax.broadcasted_iota(jnp.int32, (TOK, Q_LEN), 0) % Q_LEN
        for r in range(REQ):
            slot = OWN * GROUP + r
            keys = ql_ref[r * Q_LEN : (r + 1) * Q_LEN, 0:RANK]
            rope_k = ql_ref[r * Q_LEN : (r + 1) * Q_LEN, RANK:LATENT]
            scores = dot(qa[slot].reshape(TOK, RANK), keys, ((1,), (1,))) + dot(
                qrope[slot].reshape(TOK, ROPE), rope_k, ((1,), (1,))
            )
            weights, scale, as_row = softmax(jnp.where(key_at <= query_at, scores, LOWEST))
            lses[OWN, r // CAP, r % CAP : r % CAP + 1] = as_row
            finish(slot, r, weights, scale, keys)

        def store(first, values):
            vals[OWN, :, :, first : first + VDIM] = values.reshape(NX, ROWS, VDIM)

        project(OWN, store)

    key_place = lax.broadcasted_iota(jnp.int32, (1, DOC_LEN), 1)

    def attend(rel):
        owner = (z + rel) % NZ

        def quad(g, carry):
            jobs = []
            for i in range(4):
                source, turn = g * 2 + i // CAP, i % CAP
                first = x * ROWS + turn * Q_LEN
                doc = sm_got[source, owner, 0, TOK + first]
                blocks = sm_got[source, owner, 0, 2 * TOK + first]
                index = g * 4 + i
                slot = rel * GROUP + index
                scores = dot(qa[slot].reshape(TOK, RANK), full[doc, :, 0:RANK], ((1,), (1,))) + dot(
                    qrope[slot].reshape(TOK, ROPE), full[doc, :, RANK:LATENT], ((1,), (1,))
                )
                jobs.append((source, turn, doc, blocks, index, slot, scores))
            soft = []
            for source, turn, doc, blocks, index, slot, scores in jobs:
                hide = jnp.where(key_place < blocks * BLOCK, 0.0, LOWEST)
                soft.append(softmax(scores + hide))
            for (source, turn, doc, blocks, index, slot, scores), (weights, scale, as_row) in zip(jobs, soft):
                lses[rel, source, turn : turn + 1] = as_row
                finish(slot, index, weights, scale, full[doc, :, 0:RANK])
            return carry

        lax.fori_loop(0, GROUP // 4, quad, 0)

        def store(first, values):
            vals[rel, :, :, first : first + VDIM] = values.reshape(NX, ROWS, VDIM)

        project(rel, store)

    returning = {}

    def hand_over(rel):
        returning[rel] = []
        for j in range(1, NX):
            peer = (x + j) % NX
            returning[rel] += [
                remote(vals.at[rel, peer], xv.at[rel, x], vs.at[rel, j], vr.at[rel, j], x_peer[j]),
                remote(lses.at[rel, peer], xl.at[rel, x], es.at[rel, j], er.at[rel, j], x_peer[j]),
            ]
        xv[rel, pl.ds(x, 1)] = vals[rel, pl.ds(x, 1)]
        xl[rel, pl.ds(x, 1)] = lses[rel, pl.ds(x, 1)]

    request_at = lax.broadcasted_iota(jnp.int32, (REQ, TOK), 0) * Q_LEN

    def merge(rel, partials, store):
        for copy in returning[rel]:
            copy.wait_recv()
        owner = (z + rel) % NZ
        pick = picked(rel)
        hits, rows = [], []
        for s in range(GROUP):
            hits.append(request_at == sm_own[owner, 0, s * Q_LEN])
            rows.append(xl[rel, s // CAP, s % CAP : s % CAP + 1])
        top = jnp.full((REQ, TOK), LOWEST, F32)
        for _, lse in partials:
            top = jnp.maximum(top, lse)
        for hit, lse in zip(hits, rows):
            top = jnp.maximum(top, jnp.where(hit, lse, LOWEST))
        part_share = [jnp.exp(lse - top) for _, lse in partials]
        slot_share = [jnp.where(hit, jnp.exp(lse - top), 0.0) for hit, lse in zip(hits, rows)]
        total = jnp.maximum(sum(part_share + slot_share), 1e-30)
        scale = 1.0 / total
        shares = [share * scale for share in part_share] + [
            jnp.sum(share * scale, axis=0, keepdims=True) for share in slot_share
        ]
        turned = jnp.transpose(jnp.concatenate(shares, axis=0))
        count = len(partials)
        for head in range(HD):
            mine = turned[head * Q_LEN : (head + 1) * Q_LEN]

            def stacked(first):
                return jnp.concatenate([mine[:, k : k + 1] for k in range(first, first + REQ)], axis=0)

            at = head * VDIM
            slot_values = xv[rel, :, :, at : at + VDIM].reshape(TOK, VDIM).astype(F32)
            scaled = (slot_values * stacked(count * REQ)).astype(BF16)
            result = dot(pick, scaled, ((1,), (0,)))
            for k, (values, _) in enumerate(partials):
                result = result + values(at).astype(F32) * stacked(k * REQ)
            store(at, result.astype(BF16))
        return top + jnp.log(total)

    def incoming(i):
        return (lambda at: inv_v[i, :, at : at + VDIM]), in_l[i].reshape(REQ, TOK)

    falling = {}

    def pass_on(rel, span, span_l, target, i, peer):
        falling[i] = [
            remote(pv.at[rel, span], inv_v.at[target, span], ps.at[i], pr.at[i], peer),
            remote(plse.at[rel, span_l], in_l.at[target, span_l], fs.at[i], fr.at[i], peer),
        ]

    def settle(rel, awaited):
        partials = []
        if awaited is not None:
            for copy in falling[awaited]:
                copy.wait_recv()
            partials = [incoming(rel)]

        def store(at, values):
            pv[rel, :, at : at + VDIM] = values

        plse[rel] = merge(rel, partials, store).reshape(2, REQ // 2, TOK)

    everything, both = pl.ds(0, TOK), pl.ds(0, 2)
    inv_v[3, half:TOK] = jnp.zeros((half, VW), BF16)
    inv_v[5, 0:half] = jnp.zeros((half, VW), BF16)
    in_l[3, 1] = jnp.full((REQ // 2, TOK), LOWEST, F32)
    in_l[5, 0] = jnp.full((REQ // 2, TOK), LOWEST, F32)

    forward(0)
    own_term()
    ring_a.wait_recv()
    ring_a = ring(2, gq.at[7], gq.at[6], right)
    ring_b.wait_recv()
    ring_b = ring(3, gq.at[1], gq.at[2], left)
    forward(7)
    forward(1)
    take_in(0)
    for copy in passed:
        copy.wait_recv()
    got_table = pltpu.make_async_copy(tblx, sm_got, ls.at[2])
    got_table.start()
    ring_a.wait_recv()
    ring_a = ring(4, gq.at[6], gq.at[5], right)
    ring_b.wait_recv()
    ring_b = ring(5, gq.at[2], gq.at[3], left)
    forward(6)
    forward(2)
    take_in(7)
    take_in(1)
    ring_a.wait_recv()
    ring_a = ring(6, gq.at[5, low], gq.at[4, low], right)
    ring_b.wait_recv()
    ring_b = ring(7, gq.at[3, high], gq.at[4, high], left)
    forward(5)
    forward(3)
    take_in(6)
    take_in(2)

    docs_up.wait_recv()
    pass_up = remote(part(h_down, 0), part(h_down, 0), ys.at[2], yr.at[2], up)
    cross_down = remote(place(h_down), place(h_down), cs.at[1], cr.at[1], other)
    docs_down.wait_recv()
    pass_down = remote(part(h_up, 8), part(h_up, 8), ys.at[3], yr.at[3], down)
    cross_up = remote(place(h_up), place(h_up), cs.at[2], cr.at[2], other)

    ring_a.wait_recv()
    ring_b.wait_recv()
    forward(4)
    take_in(5)
    take_in(3)

    pass_up.wait_recv()
    pass_down.wait_recv()
    cross_far = remote(place(h_far), place(h_far), cs.at[3], cr.at[3], other)
    take_in(4)
    own_docs.wait()
    own_table.wait()
    got_table.wait()
    for copy in (docs_other, cross_down, cross_up, cross_far):
        copy.wait_recv()

    attend(4)
    hand_over(4)
    attend(3)
    hand_over(3)
    settle(4, None)
    pass_on(4, low, pl.ds(0, 1), 3, 0, right)
    pass_on(4, high, pl.ds(1, 1), 5, 1, left)
    attend(5)
    hand_over(5)
    settle(3, 0)
    pass_on(3, everything, both, 2, 2, right)
    attend(2)
    hand_over(2)
    settle(5, 1)
    pass_on(5, everything, both, 6, 3, left)
    attend(6)
    hand_over(6)
    settle(2, 2)
    pass_on(2, everything, both, 1, 4, right)
    attend(1)
    hand_over(1)
    settle(6, 3)
    pass_on(6, everything, both, 7, 5, left)
    attend(7)
    hand_over(7)
    settle(1, 4)
    pass_on(1, everything, both, 0, 6, right)
    attend(0)
    hand_over(0)
    settle(7, 5)
    pass_on(7, everything, both, 4, 7, left)
    for copy in falling[6] + falling[7]:
        copy.wait_recv()

    def own_values(at):
        return vals[OWN, :, :, at : at + VDIM].reshape(TOK, VDIM)

    def store(at, values):
        out_ref[:, at : at + VDIM] = values

    merge(0, [incoming(0), incoming(4), (own_values, lses[OWN].reshape(REQ, TOK))], store)
    for copy in sent:
        copy.wait_send()


def whole(q_nope, q_rope, question_latent, table, doc_cache, w_uk, w_uv):
    local = pl.BlockSpec(memory_space=pltpu.VMEM)
    anywhere = pl.BlockSpec(memory_space=pl.ANY)
    dma = pltpu.SemaphoreType.DMA
    return pl.pallas_call(
        whole_kernel,
        out_shape=jax.ShapeDtypeStruct((TOK, VW), BF16),
        in_specs=[local, local, local, local, anywhere, local, local],
        out_specs=local,
        scratch_shapes=[
            pltpu.VMEM((DOC_DEV, DOC_LEN, LATENT), BF16),
            pltpu.VMEM((NZ, TOK, QW), BF16),
            pltpu.VMEM((NZ, NX, ROWS, QW), BF16),
            pltpu.VMEM((NZ, NX, ROWS, QW), BF16),
            pltpu.VMEM((NZ, 1, TBL), jnp.int32),
            pltpu.VMEM((NX, NZ, 1, TBL), jnp.int32),
            pltpu.SMEM((NZ, 1, TBL), jnp.int32),
            pltpu.SMEM((NX, NZ, 1, TBL), jnp.int32),
            pltpu.VMEM(((NZ + 1) * GROUP, HD, Q_LEN, RANK), BF16),
            pltpu.VMEM(((NZ + 1) * GROUP, HD, Q_LEN, ROPE), BF16),
            pltpu.VMEM((GROUP, HD, Q_LEN, VDIM), F32),
            pltpu.VMEM((NZ + 1, NX, ROWS, VW), BF16),
            pltpu.VMEM((NZ + 1, NX, CAP, TOK), F32),
            pltpu.VMEM((NZ, NX, ROWS, VW), BF16),
            pltpu.VMEM((NZ, NX, CAP, TOK), F32),
            pltpu.VMEM((NZ, TOK, VW), BF16),
            pltpu.VMEM((NZ, 2, REQ // 2, TOK), F32),
            pltpu.VMEM((NZ, TOK, VW), BF16),
            pltpu.VMEM((NZ, 2, REQ // 2, TOK), F32),
            dma((8,)), dma((8,)),
            dma((NZ,)), dma((NZ,)),
            dma((NX,)), dma((NX,)),
            dma((NZ, NX)), dma((NZ, NX)),
            dma((4,)), dma((4,)),
            dma((4,)), dma((4,)),
            dma((NZ, NX)), dma((NZ, NX)),
            dma((NZ, NX)), dma((NZ, NX)),
            dma((8,)), dma((8,)),
            dma((8,)), dma((8,)),
            dma((3,)),
        ],
        compiler_params=pltpu.CompilerParams(
            collective_id=0, has_side_effects=True, vmem_limit_bytes=VMEM_LIMIT
        ),
        name="whole",
    )(q_nope, q_rope, question_latent, table, doc_cache, w_uk, w_uv)


def on_device(
    q_nope, q_rope, question_latent, doc_cache, w_uk, w_uv, doc_slot, doc_blocks, pair_doc, pair_req
):
    doc_ids = jnp.arange(doc_slot.shape[0], dtype=jnp.int32)
    matches = pair_doc[:, None] == doc_ids[None, :]
    pair_slot = jnp.sum(jnp.where(matches, doc_slot[None, :], 0), axis=1)
    pair_blocks = jnp.sum(jnp.where(matches, doc_blocks[None, :], 0), axis=1)
    target = pair_slot // DOC_DEV
    sequence = jnp.arange(PAIRS, dtype=jnp.int32)
    before = (target[:, None] == target[None, :]) & (sequence[None, :] < sequence[:, None])
    position = target * CAP + jnp.sum(before.astype(jnp.int32), axis=1)
    placed = jnp.arange(SLOTS, dtype=jnp.int32)[:, None] == position[None, :]

    def per_slot(values):
        return jnp.sum(jnp.where(placed, values[None, :], 0), axis=1)[:, None]

    first_token = per_slot(pair_req * Q_LEN + 1) - 1
    places = jnp.arange(Q_LEN, dtype=jnp.int32)
    tokens = jnp.where(first_token >= 0, first_token + places, -1)
    doc = jnp.broadcast_to(per_slot(pair_slot % DOC_DEV), (SLOTS, Q_LEN))
    blocks = jnp.broadcast_to(per_slot(pair_blocks), (SLOTS, Q_LEN))
    table = jnp.concatenate(
        [part.reshape(NZ, 1, NX * ROWS) for part in (tokens, doc, blocks)], axis=2
    )
    return whole(q_nope, q_rope, question_latent, table, doc_cache, w_uk, w_uv)


def solution(mesh):
    placed = (
        P("doc", "head"),
        P("doc", "head"),
        P("doc", None),
        P("doc", "head", None),
        P("head", None, None),
        P("head", None, None),
        P(),
        P(),
        P("doc"),
        P("doc"),
    )
    return jax.shard_map(
        on_device, mesh=mesh, in_specs=placed, out_specs=P("doc", "head"), check_vma=False
    )
```

```python
import jax
import jax.numpy as jnp
from jax import lax
from jax.experimental import pallas as pl
from jax.experimental.pallas import tpu as pltpu
from jax.sharding import PartitionSpec as P

RANK = 512
ROPE = 64
NOPE = 128
VDIM = 128
LATENT = RANK + ROPE
Q_LEN = 16
BLOCK = 128
DOC_LEN = 512
HD = 8
TOK = 128
REQ = 8
DOC_DEV = 16
PAIRS = 32
CAP = 2
ROWS = CAP * Q_LEN
NX, NZ, NY = 4, 8, 4
N_DOC = NX * NZ
SLOTS = N_DOC * CAP
GROUP = NX * CAP
CHUNKS = 4
HALVES = 2
OWN = NZ
NW = HD * NOPE
QW = HD * (NOPE + ROPE)
VW = HD * VDIM
POS = 64
LANES = 128
TBL = 3 * NX * ROWS
SCALE = (NOPE + ROPE) ** (-0.5)
LN2 = 0.6931471805599453
EXP2_SCALE = SCALE / LN2
LOWEST = -1e30
MESH = pl.DeviceIdType.MESH
F32 = jnp.float32
BF16 = jnp.bfloat16
VMEM_LIMIT = 58 * 1024 * 1024


def dot(a, b, dims):
    return lax.dot_general(a, b, (dims, ((), ())), preferred_element_type=F32)


def whole_kernel(
    qn_ref, qr_ref, qlt_ref, doc_ref, uk_hbm, uv_hbm, slot_ref, blocks_ref, name_ref, request_ref, out_ref,
    full_lat, full_rope, doc_in, uk_ref, uv_ref, ql, gq, sendb, slots, tbl, tblb, tblx, sm_own, sm_got,
    qa, q_lo, q_hi, inv, vals, lses, xv, xl, pv, plse, in_v, in_l,
    zs, zr, ts, tr, us, ur, xs, xr, ys, yr, cs, cr, vs, vr, es, er, ps, pr, fs, fr, ls,
):
    d = lax.axis_index("doc")
    h = lax.axis_index("head")
    z, x = d // NX, d % NX
    y, c = h // 2, h % 2
    z_peer = [None] + [(((z + j) % NZ) * NX + x, h) for j in range(1, NZ)]
    x_peer = [None] + [(z * NX + (x + j) % NX, h) for j in range(1, NX)]
    right, left = z_peer[1], z_peer[NZ - 1]
    h_up = ((y + 1) % NY) * 2 + c
    h_down = ((y + NY - 1) % NY) * 2 + c
    h_far = ((y + 2) % NY) * 2 + c
    up, down, other = (d, h_up), (d, h_down), (d, y * 2 + 1 - c)

    barrier = pltpu.get_barrier_semaphore()
    greeted = z_peer[1:] + x_peer[1:] + [up, down, other]
    for peer in greeted:
        pl.semaphore_signal(barrier, inc=1, device_id=peer, device_id_type=MESH)

    def here(src, dst, i):
        copy = pltpu.make_async_copy(src, dst, ls.at[i])
        copy.start()
        return copy

    doc_lat = doc_ref.at[:, :, :, pl.ds(0, RANK)]

    def lat(head, first=0, count=DOC_DEV):
        return full_lat.at[pl.ds(first, count), :, head]

    def rope(head, first=0, count=DOC_DEV):
        return full_rope.at[pl.ds(first, count), head]

    queries_in = [
        here(qn_ref, gq.at[0, :, pl.ds(0, NW)], 0),
        here(qr_ref, gq.at[0, :, pl.ds(NW, QW - NW)], 1),
    ]
    docs_in = here(doc_ref, doc_in, 2)
    own_lat = here(doc_lat, lat(h), 3)
    weights_in = [here(uk_hbm, uk_ref, 4), here(uv_hbm, uv_ref, 5)]
    for copy in queries_in:
        copy.wait()
    pl.semaphore_wait(barrier, len(greeted))

    sent = []

    def remote(src, dst, send, recv, peer):
        copy = pltpu.make_async_remote_copy(
            src_ref=src, dst_ref=dst, send_sem=send, recv_sem=recv, device_id=peer, device_id_type=MESH
        )
        copy.start()
        sent.append(copy)
        return copy

    half = TOK // 2
    low, high = pl.ds(0, half), pl.ds(half, half)
    chain = ((0, 7, 6, 5, 4), (0, 1, 2, 3, 4))
    hops = {}

    def hop(way, step, k):
        rows = pl.ds(k * (TOK // CHUNKS), TOK // CHUNKS)
        hops[way, step, k] = remote(
            gq.at[chain[way][step], rows], gq.at[chain[way][step + 1], rows],
            zs.at[way, step, k], zr.at[way, step, k], (right, left)[way],
        )

    for k in range(CHUNKS):
        hop(0, 0, k)
        hop(1, 0, k)

    def advance(step):
        for k in range(CHUNKS):
            for way in range(2):
                hops[way, step - 1, k].wait_recv()
                if step < 3 or (k < CHUNKS // 2) == (way == 0):
                    hop(way, step, k)

    part = DOC_DEV // CHUNKS
    docs_up, docs_down, pass_up, pass_down, crossed = {}, {}, {}, {}, []

    def cross(src):
        i = len(crossed)
        crossed.append(remote(src, src, cs.at[i], cr.at[i], other))

    def doc_part(k):
        return doc_ref.at[pl.ds(k * part, part), :, :, pl.ds(0, RANK)]

    for e in range(CHUNKS):
        k, m = e, (e + 2) % CHUNKS
        docs_up[k] = remote(doc_part(k), lat(h, k * part, part), ys.at[0, k], yr.at[0, k], up)
        docs_down[m] = remote(doc_part(m), lat(h, m * part, part), ys.at[1, m], yr.at[1, m], down)
    crossed.append(remote(doc_lat, lat(h), cs.at[0], cr.at[0], other))

    lane = lax.broadcasted_iota(jnp.int32, (NZ, TOK), 1)
    channel = lax.broadcasted_iota(jnp.int32, (NZ, TOK), 0) * NX + lane // ROWS
    turn_at = (lane % ROWS) // Q_LEN
    token_at = lane % Q_LEN

    def route(k, carry):
        tokens, docs, blocks, filled = carry
        name = name_ref[k]
        place = slot_ref[name]
        mine = channel == place // DOC_DEV
        put = mine & (turn_at == filled)
        return (
            jnp.where(put, request_ref[k] * Q_LEN + token_at, tokens),
            jnp.where(put, place % DOC_DEV, docs),
            jnp.where(put, blocks_ref[name], blocks),
            jnp.where(mine, filled + 1, filled),
        )

    nothing = jnp.zeros((NZ, TOK), jnp.int32)
    routed = lax.fori_loop(0, PAIRS, route, (nothing - 1, nothing, nothing, nothing))
    for k in range(3):
        tbl[:, :, k * TOK : (k + 1) * TOK] = routed[k].reshape(NZ, 1, TOK)
    tables = [
        remote(tbl.at[(z + j) % NZ], tblb.at[z], ts.at[j], tr.at[j], z_peer[j]) for j in range(1, NZ)
    ]
    tblb[pl.ds(z, 1)] = tbl[pl.ds(z, 1)]

    docs_in.wait()
    packed = jnp.concatenate([doc_in[:, 0, :, RANK:LATENT], doc_in[:, 1, :, RANK:LATENT]], axis=2)
    full_rope[:, pl.ds(h, 1)] = packed.reshape(DOC_DEV, 1, POS // 2, LANES)
    rope_up = remote(rope(h), rope(h), ys.at[0, 4], yr.at[0, 4], up)
    rope_down = remote(rope(h), rope(h), ys.at[1, 4], yr.at[1, 4], down)
    cross(rope(h))

    for copy in tables:
        copy.wait_recv()
    passed = [remote(tblb, tblx.at[x], us.at[j], ur.at[j], x_peer[j]) for j in range(1, NX)]
    tblx[pl.ds(x, 1)] = tblb[...].reshape(1, NZ, 1, TBL)
    own_table = here(tblb, sm_own, 6)

    token = lax.broadcasted_iota(jnp.int32, (TOK, NX * ROWS), 0)
    arriving = {}

    def picked(rel):
        wanted = tblb[(z + rel) % NZ][:, 0:TOK]
        return jnp.where(token == wanted, 1.0, 0.0).astype(BF16)

    def forward(rel):
        pick = picked(rel)
        for k in range(0, QW, 512):
            chosen = dot(pick, gq[rel, :, k : k + 512], ((0,), (0,))).astype(BF16)
            sendb[rel, :, :, k : k + 512] = chosen.reshape(NX, ROWS, 512)
        arriving[rel] = [
            remote(
                sendb.at[rel, (x + j) % NX], slots.at[rel, x], xs.at[rel, j], xr.at[rel, j], x_peer[j]
            )
            for j in range(1, NX)
        ]
        slots[rel, pl.ds(x, 1)] = sendb[rel, pl.ds(x, 1)]

    def absorb(group, rows):
        span = pl.ds(group * GROUP, GROUP)
        blank = jnp.zeros((TOK, ROPE), BF16)
        for head in range(HD):
            nope = rows(head * NOPE, NOPE).reshape(TOK, NOPE)
            absorbed = dot(nope, uk_ref[head], ((1,), (0,))).astype(BF16)
            qa[span, head] = absorbed.reshape(GROUP, Q_LEN, RANK)
            turned = rows(NW + head * ROPE, ROPE).reshape(TOK, ROPE)
            q_lo[span, head] = jnp.concatenate([turned, blank], axis=1).reshape(GROUP, Q_LEN, LANES)
            q_hi[span, head] = jnp.concatenate([blank, turned], axis=1).reshape(GROUP, Q_LEN, LANES)

    def take_in(rel):
        for copy in arriving[rel]:
            copy.wait_recv()
        absorb(rel, lambda first, width: slots[rel, :, :, first : first + width])

    row = lax.broadcasted_iota(jnp.int32, (TOK, TOK), 0)
    column = lax.broadcasted_iota(jnp.int32, (TOK, TOK), 1)
    diagonal = row == column

    def softmax(scores):
        largest = jnp.max(scores, axis=1, keepdims=True) * EXP2_SCALE
        weights = jnp.exp2(scores * EXP2_SCALE - largest)
        totals = jnp.sum(weights, axis=1, keepdims=True)
        lse = largest * LN2 + jnp.log(totals)
        as_row = jnp.sum(jnp.where(diagonal, lse, 0.0), axis=0, keepdims=True)
        return weights.astype(BF16), 1.0 / totals, as_row

    def finish(slot, i, weights, scale, keys):
        latent = dot(weights, keys, ((1,), (0,)))
        qa[slot] = latent.astype(BF16).reshape(HD, Q_LEN, RANK)
        inv[i] = jnp.broadcast_to(scale, (TOK, VDIM)).reshape(HD, Q_LEN, VDIM)

    def project(group, part_of):
        for j in range(HD // HALVES):
            head = part_of * (HD // HALVES) + j
            latent = qa[pl.ds(group * GROUP, GROUP), head].reshape(TOK, RANK)
            values = dot(latent, uv_ref[head], ((1,), (0,))) * inv[:, head].reshape(TOK, VDIM)
            vals[group, part_of, :, :, j * VDIM : (j + 1) * VDIM] = values.astype(BF16).reshape(
                NX, ROWS, VDIM
            )

    def own_term():
        for k in range(0, LATENT, LANES):
            width = min(LANES, LATENT - k)
            ql[:, k : k + width] = jnp.transpose(qlt_ref[k : k + width].astype(F32)).astype(BF16)
        absorb(OWN, lambda first, width: gq[0, :, first : first + width])
        key_at = lax.broadcasted_iota(jnp.int32, (TOK, Q_LEN), 1)
        query_at = lax.broadcasted_iota(jnp.int32, (TOK, Q_LEN), 0) % Q_LEN
        for r in range(REQ):
            slot = OWN * GROUP + r
            keys = ql[r * Q_LEN : (r + 1) * Q_LEN, 0:RANK]
            rope_k = ql[r * Q_LEN : (r + 1) * Q_LEN, RANK:LATENT]
            turned = q_lo[slot].reshape(TOK, LANES)[:, 0:ROPE]
            scores = dot(qa[slot].reshape(TOK, RANK), keys, ((1,), (1,))) + dot(
                turned, rope_k, ((1,), (1,))
            )
            weights, scale, as_row = softmax(jnp.where(key_at <= query_at, scores, LOWEST))
            lses[OWN, r // CAP, r % CAP : r % CAP + 1] = as_row
            finish(slot, r, weights, scale, keys)
        for p in range(HALVES):
            project(OWN, p)

    key_block = lax.broadcasted_iota(jnp.int32, (1, DOC_LEN), 1) % (DOC_LEN // 2) // (BLOCK // 2)
    returning = {}

    def attend(rel):
        owner = (z + rel) % NZ

        def quad(g, carry):
            jobs = []
            for i in range(4):
                source, turn = g * 2 + i // CAP, i % CAP
                first = x * ROWS + turn * Q_LEN
                doc = sm_got[source, owner, 0, TOK + first]
                blocks = sm_got[source, owner, 0, 2 * TOK + first]
                index = g * 4 + i
                slot = rel * GROUP + index
                keys = full_lat[doc].reshape(DOC_LEN, RANK)
                turned = full_rope[doc].reshape(DOC_LEN // 2, LANES)
                scores = dot(qa[slot].reshape(TOK, RANK), keys, ((1,), (1,))) + jnp.concatenate(
                    [
                        dot(q_lo[slot].reshape(TOK, LANES), turned, ((1,), (1,))),
                        dot(q_hi[slot].reshape(TOK, LANES), turned, ((1,), (1,))),
                    ],
                    axis=1,
                )
                jobs.append((source, turn, doc, blocks, index, slot, scores))
            soft = []
            for source, turn, doc, blocks, index, slot, scores in jobs:
                hide = jnp.where(key_block < blocks, 0.0, LOWEST)
                soft.append(softmax(scores + hide))
            for (source, turn, doc, blocks, index, slot, scores), (weights, scale, as_row) in zip(jobs, soft):
                lses[rel, source, turn : turn + 1] = as_row
                finish(slot, index, weights, scale, full_lat[doc].reshape(DOC_LEN, RANK))
            return carry

        lax.fori_loop(0, GROUP // 4, quad, 0)
        returning[rel] = [
            [
                remote(lses.at[rel, (x + j) % NX], xl.at[rel, x], es.at[rel, j], er.at[rel, j], x_peer[j])
                for j in range(1, NX)
            ]
        ]
        xl[rel, pl.ds(x, 1)] = lses[rel, pl.ds(x, 1)]
        for p in range(HALVES):
            project(rel, p)
            returning[rel].append(
                [
                    remote(
                        vals.at[rel, p, (x + j) % NX], xv.at[rel, p, x],
                        vs.at[rel, p, j], vr.at[rel, p, j], x_peer[j],
                    )
                    for j in range(1, NX)
                ]
            )
            xv[rel, p, pl.ds(x, 1)] = vals[rel, p, pl.ds(x, 1)]

    request_at = lax.broadcasted_iota(jnp.int32, (REQ, TOK), 0) * Q_LEN

    def merge(rel, partials, lse_done, half_ready, store, half_done):
        owner = (z + rel) % NZ
        pick = picked(rel)
        for copy in returning[rel][0]:
            copy.wait_recv()
        hits, rows = [], []
        for s in range(GROUP):
            hits.append(request_at == sm_own[owner, 0, s * Q_LEN])
            rows.append(xl[rel, s // CAP, s % CAP : s % CAP + 1])
        top = jnp.full((REQ, TOK), LOWEST, F32)
        for _, lse in partials:
            top = jnp.maximum(top, lse)
        for hit, lse in zip(hits, rows):
            top = jnp.maximum(top, jnp.where(hit, lse, LOWEST))
        part_share = [jnp.exp(lse - top) for _, lse in partials]
        slot_share = [jnp.where(hit, jnp.exp(lse - top), 0.0) for hit, lse in zip(hits, rows)]
        total = jnp.maximum(sum(part_share + slot_share), 1e-30)
        lse_done(top + jnp.log(total))
        scale = 1.0 / total
        shares = [share * scale for share in part_share] + [
            jnp.sum(share * scale, axis=0, keepdims=True) for share in slot_share
        ]
        turned = jnp.transpose(jnp.concatenate(shares, axis=0))
        count = len(partials)
        for p in range(HALVES):
            for copy in returning[rel][1 + p]:
                copy.wait_recv()
            half_ready(p)
            for j in range(HD // HALVES):
                head = p * (HD // HALVES) + j
                mine = turned[head * Q_LEN : (head + 1) * Q_LEN]

                def stacked(first):
                    return jnp.concatenate([mine[:, k : k + 1] for k in range(first, first + REQ)], axis=0)

                at = j * VDIM
                slot_values = xv[rel, p, :, :, at : at + VDIM].reshape(TOK, VDIM).astype(F32)
                scaled = (slot_values * stacked(count * REQ)).astype(BF16)
                result = dot(pick, scaled, ((1,), (0,)))
                for k, (values, _) in enumerate(partials):
                    result = result + values(p, at).astype(F32) * stacked(k * REQ)
                store(p, at, result.astype(BF16))
            half_done(p)

    def incoming(i):
        return (lambda p, at: in_v[i, p, :, at : at + VDIM]), in_l[i].reshape(REQ, TOK)

    falling_l, falling_v = {}, {}
    everything, both = pl.ds(0, TOK), pl.ds(0, 2)

    def settle(rel, awaited, moves):
        def lse_done(lse):
            plse[rel] = lse.reshape(2, REQ // 2, TOK)
            for i, target, span, span_l, peer in moves:
                falling_l[i] = remote(
                    plse.at[rel, span_l], in_l.at[target, span_l], fs.at[i], fr.at[i], peer
                )

        def half_ready(p):
            if awaited is not None:
                falling_v[awaited, p].wait_recv()

        def store(p, at, values):
            pv[rel, p, :, at : at + VDIM] = values

        def half_done(p):
            for i, target, span, span_l, peer in moves:
                falling_v[i, p] = remote(
                    pv.at[rel, p, span], in_v.at[target, p, span], ps.at[i, p], pr.at[i, p], peer
                )

        partials = []
        if awaited is not None:
            falling_l[awaited].wait_recv()
            partials = [incoming(rel)]
        merge(rel, partials, lse_done, half_ready, store, half_done)

    in_v[3, :, half:TOK] = jnp.zeros((HALVES, half, VW // HALVES), BF16)
    in_v[5, :, 0:half] = jnp.zeros((HALVES, half, VW // HALVES), BF16)
    in_l[3, 1] = jnp.full((REQ // 2, TOK), LOWEST, F32)
    in_l[5, 0] = jnp.full((REQ // 2, TOK), LOWEST, F32)

    def docs_event(e):
        k, m = e, (e + 2) % CHUNKS
        docs_up[k].wait_recv()
        if e < CHUNKS // 2:
            span = lat(h_down, k * part, part)
            pass_up[e] = remote(span, span, ys.at[0, 5 + e], yr.at[0, 5 + e], up)
        cross(lat(h_down, k * part, part))
        docs_down[m].wait_recv()
        if e < CHUNKS // 2:
            span = lat(h_up, m * part, part)
            pass_down[e] = remote(span, span, ys.at[1, 5 + e], yr.at[1, 5 + e], down)
        cross(lat(h_up, m * part, part))

    forward(0)
    for copy in weights_in:
        copy.wait()
    own_term()
    advance(1)
    forward(7)
    forward(1)
    docs_event(0)
    take_in(0)
    for copy in passed:
        copy.wait_recv()
    got_table = here(tblx, sm_got, 7)
    advance(2)
    docs_event(1)
    forward(6)
    forward(2)
    take_in(7)
    take_in(1)
    docs_event(2)
    advance(3)
    forward(5)
    forward(3)
    docs_event(3)
    rope_up.wait_recv()
    span = rope(h_down, 0, DOC_DEV // 2)
    pass_up[2] = remote(span, span, ys.at[0, 7], yr.at[0, 7], up)
    cross(rope(h_down))
    rope_down.wait_recv()
    span = rope(h_up, DOC_DEV // 2, DOC_DEV // 2)
    pass_down[2] = remote(span, span, ys.at[1, 7], yr.at[1, 7], down)
    cross(rope(h_up))
    take_in(6)
    take_in(2)
    for k in range(CHUNKS):
        hops[k * 2 // CHUNKS, 3, k].wait_recv()
    forward(4)
    take_in(5)
    take_in(3)
    for e in range(CHUNKS // 2):
        pass_up[e].wait_recv()
        cross(lat(h_far, e * part, part))
        pass_down[e].wait_recv()
        cross(lat(h_far, (e + 2) * part, part))
    take_in(4)
    pass_up[2].wait_recv()
    cross(rope(h_far, 0, DOC_DEV // 2))
    pass_down[2].wait_recv()
    cross(rope(h_far, DOC_DEV // 2, DOC_DEV // 2))
    own_lat.wait()
    own_table.wait()
    got_table.wait()
    for copy in crossed:
        copy.wait_recv()

    attend(4)
    attend(3)
    settle(4, None, [(0, 3, low, pl.ds(0, 1), right), (1, 5, high, pl.ds(1, 1), left)])
    attend(5)
    settle(3, 0, [(2, 2, everything, both, right)])
    attend(2)
    settle(5, 1, [(3, 6, everything, both, left)])
    attend(6)
    settle(2, 2, [(4, 1, everything, both, right)])
    attend(1)
    settle(6, 3, [(5, 7, everything, both, left)])
    attend(7)
    settle(1, 4, [(6, 0, everything, both, right)])
    attend(0)
    settle(7, 5, [(7, 4, everything, both, left)])

    def own_values(p, at):
        return vals[OWN, p, :, :, at : at + VDIM].reshape(TOK, VDIM)

    def last_ready(p):
        falling_v[6, p].wait_recv()
        falling_v[7, p].wait_recv()

    def store(p, at, values):
        first = p * (VW // HALVES) + at
        out_ref[:, first : first + VDIM] = values

    def done(_):
        return None

    falling_l[6].wait_recv()
    falling_l[7].wait_recv()
    merge(
        0, [incoming(0), incoming(4), (own_values, lses[OWN].reshape(REQ, TOK))],
        done, last_ready, store, done,
    )
    for copy in sent:
        copy.wait_send()


def whole(q_nope, q_rope, latent_turned, doc_cache, w_uk, w_uv, doc_slot, doc_blocks, pair_doc, pair_req):
    local = pl.BlockSpec(memory_space=pltpu.VMEM)
    anywhere = pl.BlockSpec(memory_space=pl.ANY)
    scalar = pl.BlockSpec(memory_space=pltpu.SMEM)
    dma = pltpu.SemaphoreType.DMA
    return pl.pallas_call(
        whole_kernel,
        out_shape=jax.ShapeDtypeStruct((TOK, VW), BF16),
        in_specs=[anywhere, anywhere, local, anywhere, anywhere, anywhere] + [scalar] * 4,
        out_specs=local,
        scratch_shapes=[
            pltpu.VMEM((DOC_DEV, 2, HD, POS // 2, RANK), BF16),
            pltpu.VMEM((DOC_DEV, HD, POS // 2, LANES), BF16),
            pltpu.VMEM((DOC_DEV, 2, POS // 2, LATENT), BF16),
            pltpu.VMEM((HD, NOPE, RANK), BF16),
            pltpu.VMEM((HD, RANK, VDIM), BF16),
            pltpu.VMEM((TOK, LATENT), BF16),
            pltpu.VMEM((NZ, TOK, QW), BF16),
            pltpu.VMEM((NZ, NX, ROWS, QW), BF16),
            pltpu.VMEM((NZ, NX, ROWS, QW), BF16),
            pltpu.VMEM((NZ, 1, TBL), jnp.int32),
            pltpu.VMEM((NZ, 1, TBL), jnp.int32),
            pltpu.VMEM((NX, NZ, 1, TBL), jnp.int32),
            pltpu.SMEM((NZ, 1, TBL), jnp.int32),
            pltpu.SMEM((NX, NZ, 1, TBL), jnp.int32),
            pltpu.VMEM(((NZ + 1) * GROUP, HD, Q_LEN, RANK), BF16),
            pltpu.VMEM(((NZ + 1) * GROUP, HD, Q_LEN, LANES), BF16),
            pltpu.VMEM(((NZ + 1) * GROUP, HD, Q_LEN, LANES), BF16),
            pltpu.VMEM((GROUP, HD, Q_LEN, VDIM), F32),
            pltpu.VMEM((NZ + 1, HALVES, NX, ROWS, VW // HALVES), BF16),
            pltpu.VMEM((NZ + 1, NX, CAP, TOK), F32),
            pltpu.VMEM((NZ, HALVES, NX, ROWS, VW // HALVES), BF16),
            pltpu.VMEM((NZ, NX, CAP, TOK), F32),
            pltpu.VMEM((NZ, HALVES, TOK, VW // HALVES), BF16),
            pltpu.VMEM((NZ, 2, REQ // 2, TOK), F32),
            pltpu.VMEM((NZ, HALVES, TOK, VW // HALVES), BF16),
            pltpu.VMEM((NZ, 2, REQ // 2, TOK), F32),
            dma((2, 4, CHUNKS)), dma((2, 4, CHUNKS)),
            dma((NZ,)), dma((NZ,)),
            dma((NX,)), dma((NX,)),
            dma((NZ, NX)), dma((NZ, NX)),
            dma((2, 8)), dma((2, 8)),
            dma((18,)), dma((18,)),
            dma((NZ, HALVES, NX)), dma((NZ, HALVES, NX)),
            dma((NZ, NX)), dma((NZ, NX)),
            dma((8, HALVES)), dma((8, HALVES)),
            dma((8,)), dma((8,)),
            dma((8,)),
        ],
        compiler_params=pltpu.CompilerParams(
            collective_id=0, has_side_effects=True, vmem_limit_bytes=VMEM_LIMIT
        ),
        name="whole",
    )(q_nope, q_rope, latent_turned, doc_cache, w_uk, w_uv, doc_slot, doc_blocks, pair_doc, pair_req)


def on_device(
    q_nope, q_rope, question_latent, doc_cache, w_uk, w_uv, doc_slot, doc_blocks, pair_doc, pair_req
):
    return whole(
        q_nope, q_rope, question_latent.T, doc_cache.reshape(DOC_DEV, 2, POS // 2, LATENT),
        w_uk, w_uv, doc_slot, doc_blocks, pair_doc, pair_req,
    )


def solution(mesh):
    placed = (
        P("doc", "head"),
        P("doc", "head"),
        P("doc", None),
        P("doc", "head", None),
        P("head", None, None),
        P("head", None, None),
        P(),
        P(),
        P("doc"),
        P("doc"),
    )
    return jax.shard_map(
        on_device, mesh=mesh, in_specs=placed, out_specs=P("doc", "head"), check_vma=False
    )
```

```python
import jax
import jax.numpy as jnp
from jax import lax
from jax.experimental import pallas as pl
from jax.experimental.pallas import tpu as pltpu
from jax.sharding import PartitionSpec as P

RANK = 512
ROPE = 64
NOPE = 128
VDIM = 128
LATENT = RANK + ROPE
Q_LEN = 16
BLOCK = 128
DOC_LEN = 512
HD = 8
TOK = 128
REQ = 8
DOC_DEV = 16
PAIRS = 32
CAP = 2
ROWS = CAP * Q_LEN
NX, NZ, NY = 4, 8, 4
N_DOC = NX * NZ
SLOTS = N_DOC * CAP
GROUP = NX * CAP
CHUNKS = 4
HALVES = 2
QUARTERS = 4
VQ = HD * VDIM // QUARTERS
OWN = NZ
NW = HD * NOPE
QW = HD * (NOPE + ROPE)
VW = HD * VDIM
POS = 64
LANES = 128
TBL = 3 * NX * ROWS
SCALE = (NOPE + ROPE) ** (-0.5)
LN2 = 0.6931471805599453
EXP2_SCALE = SCALE / LN2
LOWEST = -1e30
MESH = pl.DeviceIdType.MESH
F32 = jnp.float32
BF16 = jnp.bfloat16
VMEM_LIMIT = 62 * 1024 * 1024


def dot(a, b, dims):
    return lax.dot_general(a, b, (dims, ((), ())), preferred_element_type=F32)


def whole_kernel(
    qn_ref, qr_ref, qlt_ref, doc_ref, uk_hbm, uv_hbm, slot_ref, blocks_ref, name_ref, request_ref, out_ref,
    full_lat, full_rope, kt, doc_in, uk_ref, uv_ref, ql, gq, sendb, slots, tbl, tblb, tblx, sm_own, sm_got,
    qa, q_rope, inv, vals, lses, xv, xl, pv, plse, in_v, in_l,
    zs, zr, ts, tr, us, ur, xs, xr, ys, yr, cs, cr, vs, vr, es, er, ps, pr, fs, fr, ls,
):
    d = lax.axis_index("doc")
    h = lax.axis_index("head")
    z, x = d // NX, d % NX
    y, c = h // 2, h % 2
    z_peer = [None] + [(((z + j) % NZ) * NX + x, h) for j in range(1, NZ)]
    x_peer = [None] + [(z * NX + (x + j) % NX, h) for j in range(1, NX)]
    right, left = z_peer[1], z_peer[NZ - 1]
    h_up = ((y + 1) % NY) * 2 + c
    h_down = ((y + NY - 1) % NY) * 2 + c
    h_far = ((y + 2) % NY) * 2 + c
    up, down, other = (d, h_up), (d, h_down), (d, y * 2 + 1 - c)

    barrier = pltpu.get_barrier_semaphore()
    greeted = z_peer[1:] + x_peer[1:] + [up, down, other]
    for peer in greeted:
        pl.semaphore_signal(barrier, inc=1, device_id=peer, device_id_type=MESH)

    def here(src, dst, i):
        copy = pltpu.make_async_copy(src, dst, ls.at[i])
        copy.start()
        return copy

    doc_lat = doc_ref.at[:, :, :, pl.ds(0, RANK)]

    def lat(head, first=0, count=DOC_DEV):
        return full_lat.at[pl.ds(first, count), head // 2, :, head % 2]

    def rope(head, first=0, count=DOC_DEV):
        return full_rope.at[pl.ds(first, count), head // 2, head % 2]

    queries_in = [
        here(qn_ref, gq.at[0, :, pl.ds(0, NW)], 0),
        here(qr_ref, gq.at[0, :, pl.ds(NW, QW - NW)], 1),
    ]
    docs_in = here(doc_ref, doc_in, 2)
    own_lat = here(doc_lat, lat(h), 3)
    weights_in = [here(uk_hbm, uk_ref, 4), here(uv_hbm, uv_ref, 5)]
    lane = lax.broadcasted_iota(jnp.int32, (NZ, TOK), 1)
    channel = lax.broadcasted_iota(jnp.int32, (NZ, TOK), 0) * NX + lane // ROWS
    turn_at = (lane % ROWS) // Q_LEN
    token_at = lane % Q_LEN

    def route(k, carry):
        tokens, docs, blocks, filled = carry
        name = name_ref[k]
        place = slot_ref[name]
        mine = channel == place // DOC_DEV
        put = mine & (turn_at == filled)
        return (
            jnp.where(put, request_ref[k] * Q_LEN + token_at, tokens),
            jnp.where(put, place % DOC_DEV, docs),
            jnp.where(put, blocks_ref[name], blocks),
            jnp.where(mine, filled + 1, filled),
        )

    nothing = jnp.zeros((NZ, TOK), jnp.int32)
    routed = lax.fori_loop(0, PAIRS, route, (nothing - 1, nothing, nothing, nothing))
    for k in range(3):
        tbl[:, :, k * TOK : (k + 1) * TOK] = routed[k].reshape(NZ, 1, TOK)
    for copy in queries_in:
        copy.wait()
    pl.semaphore_wait(barrier, len(greeted))

    sent = []

    def remote(src, dst, send, recv, peer):
        copy = pltpu.make_async_remote_copy(
            src_ref=src, dst_ref=dst, send_sem=send, recv_sem=recv, device_id=peer, device_id_type=MESH
        )
        copy.start()
        sent.append(copy)
        return copy

    half = TOK // 2
    low, high = pl.ds(0, half), pl.ds(half, half)
    chain = ((0, 7, 6, 5, 4), (0, 1, 2, 3, 4))
    hops = {}

    def hop(way, step, k):
        rows = pl.ds(k * (TOK // CHUNKS), TOK // CHUNKS)
        hops[way, step, k] = remote(
            gq.at[chain[way][step], rows], gq.at[chain[way][step + 1], rows],
            zs.at[way, step, k], zr.at[way, step, k], (right, left)[way],
        )

    for k in range(CHUNKS):
        hop(0, 0, k)
        hop(1, 0, k)

    def advance(step):
        for k in range(CHUNKS):
            for way in range(2):
                hops[way, step - 1, k].wait_recv()
                if step < 3 or (k < CHUNKS // 2) == (way == 0):
                    hop(way, step, k)

    part = DOC_DEV // CHUNKS
    docs_up, docs_down, pass_up, pass_down, crossed = {}, {}, {}, {}, []

    def cross(src):
        i = len(crossed)
        crossed.append(remote(src, src, cs.at[i], cr.at[i], other))

    def doc_part(k):
        return doc_ref.at[pl.ds(k * part, part), :, :, pl.ds(0, RANK)]

    for e in range(CHUNKS):
        k, m = e, (e + 2) % CHUNKS
        docs_up[k] = remote(doc_part(k), lat(h, k * part, part), ys.at[0, k], yr.at[0, k], up)
        docs_down[m] = remote(doc_part(m), lat(h, m * part, part), ys.at[1, m], yr.at[1, m], down)
    crossed.append(remote(doc_lat, lat(h), cs.at[0], cr.at[0], other))

    tables = [
        remote(tbl.at[(z + j) % NZ], tblb.at[z], ts.at[j], tr.at[j], z_peer[j]) for j in range(1, NZ)
    ]
    tblb[pl.ds(z, 1)] = tbl[pl.ds(z, 1)]

    docs_in.wait()
    packed = jnp.concatenate([doc_in[:, 0, :, RANK:LATENT], doc_in[:, 1, :, RANK:LATENT]], axis=2)
    full_rope[:, pl.ds(y, 1), pl.ds(c, 1)] = packed.reshape(DOC_DEV, 1, 1, POS // 2, LANES)
    rope_up = remote(rope(h), rope(h), ys.at[0, 4], yr.at[0, 4], up)
    rope_down = remote(rope(h), rope(h), ys.at[1, 4], yr.at[1, 4], down)
    cross(rope(h))

    for copy in tables:
        copy.wait_recv()
    passed = [remote(tblb, tblx.at[x], us.at[j], ur.at[j], x_peer[j]) for j in range(1, NX)]
    tblx[pl.ds(x, 1)] = tblb[...].reshape(1, NZ, 1, TBL)
    own_table = here(tblb, sm_own, 6)

    token = lax.broadcasted_iota(jnp.int32, (TOK, NX * ROWS), 0)
    arriving = {}

    def picked(rel):
        wanted = tblb[(z + rel) % NZ][:, 0:TOK]
        return jnp.where(token == wanted, 1.0, 0.0).astype(BF16)

    def forward(rel):
        pick = picked(rel)
        for k in range(0, QW, 512):
            chosen = dot(pick, gq[rel, :, k : k + 512], ((0,), (0,))).astype(BF16)
            sendb[rel, :, :, k : k + 512] = chosen.reshape(NX, ROWS, 512)
        arriving[rel] = [
            remote(
                sendb.at[rel, (x + j) % NX], slots.at[rel, x], xs.at[rel, j], xr.at[rel, j], x_peer[j]
            )
            for j in range(1, NX)
        ]
        slots[rel, pl.ds(x, 1)] = sendb[rel, pl.ds(x, 1)]

    def absorb(group, rows):
        span = pl.ds(group * GROUP, GROUP)
        for head in range(HD):
            nope = rows(head * NOPE, NOPE).reshape(TOK, NOPE)
            absorbed = dot(nope, uk_ref[head], ((1,), (0,))).astype(BF16)
            qa[span, head] = absorbed.reshape(GROUP, Q_LEN, RANK)
            q_rope[span, head] = rows(NW + head * ROPE, ROPE).reshape(GROUP, Q_LEN, ROPE)

    def take_in(rel):
        for copy in arriving[rel]:
            copy.wait_recv()
        absorb(rel, lambda first, width: slots[rel, :, :, first : first + width])

    row = lax.broadcasted_iota(jnp.int32, (TOK, TOK), 0)
    column = lax.broadcasted_iota(jnp.int32, (TOK, TOK), 1)
    diagonal = row == column

    def softmax(scores):
        largest = jnp.max(scores, axis=1, keepdims=True) * EXP2_SCALE
        weights = jnp.exp2(scores * EXP2_SCALE - largest)
        totals = jnp.sum(weights, axis=1, keepdims=True)
        lse = largest * LN2 + jnp.log(totals)
        as_row = jnp.sum(jnp.where(diagonal, lse, 0.0), axis=0, keepdims=True)
        return weights.astype(BF16), 1.0 / totals, as_row

    def finish(slot, i, weights, scale, keys):
        latent = dot(weights, keys, ((1,), (0,)))
        qa[slot] = latent.astype(BF16).reshape(HD, Q_LEN, RANK)
        inv[i] = jnp.broadcast_to(scale, (TOK, VDIM)).reshape(HD, Q_LEN, VDIM)

    def project(group, part_of):
        for j in range(HD // HALVES):
            head = part_of * (HD // HALVES) + j
            latent = qa[pl.ds(group * GROUP, GROUP), head].reshape(TOK, RANK)
            values = dot(latent, uv_ref[head], ((1,), (0,))) * inv[:, head].reshape(TOK, VDIM)
            vals[group, part_of, :, :, j * VDIM : (j + 1) * VDIM] = values.astype(BF16).reshape(
                NX, ROWS, VDIM
            )

    def own_term():
        for k in range(0, LATENT, LANES):
            width = min(LANES, LATENT - k)
            ql[:, k : k + width] = jnp.transpose(qlt_ref[k : k + width].astype(F32)).astype(BF16)
        absorb(OWN, lambda first, width: gq[0, :, first : first + width])
        key_at = lax.broadcasted_iota(jnp.int32, (TOK, Q_LEN), 1)
        query_at = lax.broadcasted_iota(jnp.int32, (TOK, Q_LEN), 0) % Q_LEN
        for r in range(REQ):
            slot = OWN * GROUP + r
            keys = ql[r * Q_LEN : (r + 1) * Q_LEN, 0:RANK]
            rope_k = ql[r * Q_LEN : (r + 1) * Q_LEN, RANK:LATENT]
            scores = dot(qa[slot].reshape(TOK, RANK), keys, ((1,), (1,))) + dot(
                q_rope[slot].reshape(TOK, ROPE), rope_k, ((1,), (1,))
            )
            weights, scale, as_row = softmax(jnp.where(key_at <= query_at, scores, LOWEST))
            lses[OWN, r // CAP, r % CAP : r % CAP + 1] = as_row
            finish(slot, r, weights, scale, keys)
        for p in range(HALVES):
            project(OWN, p)

    def turn(block):
        columns = pl.ds(pl.multiple_of(block * BLOCK, BLOCK), BLOCK)

        def one_doc(doc, carry):
            kt[doc, 0:RANK, columns] = jnp.transpose(full_lat[doc, block].reshape(BLOCK, RANK))
            turned = jnp.transpose(full_rope[doc, block].reshape(POS, LANES).astype(F32)).astype(BF16)
            kt[doc, RANK:LATENT, columns] = jnp.concatenate([turned[0:ROPE], turned[ROPE:LANES]], axis=1)
            return carry

        lax.fori_loop(0, DOC_DEV, one_doc, 0)

    key_block = lax.broadcasted_iota(jnp.int32, (1, DOC_LEN), 1) // BLOCK
    returning = {}

    def attend(rel):
        owner = (z + rel) % NZ
        jobs = []
        for index in range(GROUP):
            source, turn_of = index // CAP, index % CAP
            first = x * ROWS + turn_of * Q_LEN
            doc = sm_got[source, owner, 0, TOK + first]
            blocks = sm_got[source, owner, 0, 2 * TOK + first]
            slot = rel * GROUP + index
            scores = dot(qa[slot].reshape(TOK, RANK), kt[doc, 0:RANK], ((1,), (0,))) + dot(
                q_rope[slot].reshape(TOK, ROPE), kt[doc, RANK:LATENT], ((1,), (0,))
            )
            jobs.append((source, turn_of, doc, blocks, index, slot, scores))
        soft = []
        for source, turn_of, doc, blocks, index, slot, scores in jobs:
            hide = jnp.where(key_block < blocks, 0.0, LOWEST)
            soft.append(softmax(scores + hide))
        for (source, turn_of, doc, blocks, index, slot, scores), (weights, scale, as_row) in zip(jobs, soft):
            lses[rel, source, turn_of : turn_of + 1] = as_row
            finish(slot, index, weights, scale, full_lat[doc].reshape(DOC_LEN, RANK))
        returning[rel] = [
            [
                remote(lses.at[rel, (x + j) % NX], xl.at[rel, x], es.at[rel, j], er.at[rel, j], x_peer[j])
                for j in range(1, NX)
            ]
        ]
        xl[rel, pl.ds(x, 1)] = lses[rel, pl.ds(x, 1)]
        for p in range(HALVES):
            project(rel, p)
            returning[rel].append(
                [
                    remote(
                        vals.at[rel, p, (x + j) % NX], xv.at[rel, p, x],
                        vs.at[rel, p, j], vr.at[rel, p, j], x_peer[j],
                    )
                    for j in range(1, NX)
                ]
            )
            xv[rel, p, pl.ds(x, 1)] = vals[rel, p, pl.ds(x, 1)]

    request_at = lax.broadcasted_iota(jnp.int32, (REQ, TOK), 0) * Q_LEN

    def merge(rel, partials, lse_done, part_ready, store, part_done):
        owner = (z + rel) % NZ
        pick = picked(rel)
        for copy in returning[rel][0]:
            copy.wait_recv()
        hits, rows = [], []
        for s in range(GROUP):
            hits.append(request_at == sm_own[owner, 0, s * Q_LEN])
            rows.append(xl[rel, s // CAP, s % CAP : s % CAP + 1])
        top = jnp.full((REQ, TOK), LOWEST, F32)
        for _, lse in partials:
            top = jnp.maximum(top, lse)
        for hit, lse in zip(hits, rows):
            top = jnp.maximum(top, jnp.where(hit, lse, LOWEST))
        part_share = [jnp.exp(lse - top) for _, lse in partials]
        slot_share = [jnp.where(hit, jnp.exp(lse - top), 0.0) for hit, lse in zip(hits, rows)]
        total = jnp.maximum(sum(part_share + slot_share), 1e-30)
        lse_done(top + jnp.log(total))
        scale = 1.0 / total
        shares = [share * scale for share in part_share] + [
            jnp.sum(share * scale, axis=0, keepdims=True) for share in slot_share
        ]
        turned = jnp.transpose(jnp.concatenate(shares, axis=0))
        count = len(partials)
        for p in range(HALVES):
            for copy in returning[rel][1 + p]:
                copy.wait_recv()
            for j in range(HD // HALVES):
                head = p * (HD // HALVES) + j
                quarter, at_quarter = head // 2, head % 2 * VDIM
                if head % 2 == 0:
                    part_ready(quarter)
                mine = turned[head * Q_LEN : (head + 1) * Q_LEN]

                def stacked(first):
                    return jnp.concatenate([mine[:, k : k + 1] for k in range(first, first + REQ)], axis=0)

                at = j * VDIM
                slot_values = xv[rel, p, :, :, at : at + VDIM].reshape(TOK, VDIM).astype(F32)
                scaled = (slot_values * stacked(count * REQ)).astype(BF16)
                result = dot(pick, scaled, ((1,), (0,)))
                for k, (values, _) in enumerate(partials):
                    result = result + values(head).astype(F32) * stacked(k * REQ)
                store(quarter, at_quarter, result.astype(BF16))
                if head % 2 == 1:
                    part_done(quarter)

    def incoming(i):
        def values(head):
            return in_v[i, head // 2, :, head % 2 * VDIM : (head % 2 + 1) * VDIM]

        return values, in_l[i].reshape(REQ, TOK)

    falling_l, falling_v = {}, {}
    everything, both = pl.ds(0, TOK), pl.ds(0, 2)

    def settle(rel, awaited, moves):
        def lse_done(lse):
            plse[rel] = lse.reshape(2, REQ // 2, TOK)
            for i, target, span, span_l, peer in moves:
                falling_l[i] = remote(
                    plse.at[rel, span_l], in_l.at[target, span_l], fs.at[i], fr.at[i], peer
                )

        def part_ready(p):
            if awaited is not None:
                falling_v[awaited, p].wait_recv()

        def store(p, at, values):
            pv[rel, p, :, at : at + VDIM] = values

        def part_done(p):
            for i, target, span, span_l, peer in moves:
                falling_v[i, p] = remote(
                    pv.at[rel, p, span], in_v.at[target, p, span], ps.at[i, p], pr.at[i, p], peer
                )

        partials = []
        if awaited is not None:
            falling_l[awaited].wait_recv()
            partials = [incoming(rel)]
        merge(rel, partials, lse_done, part_ready, store, part_done)

    in_v[3, :, half:TOK] = jnp.zeros((QUARTERS, half, VQ), BF16)
    in_v[5, :, 0:half] = jnp.zeros((QUARTERS, half, VQ), BF16)
    in_l[3, 1] = jnp.full((REQ // 2, TOK), LOWEST, F32)
    in_l[5, 0] = jnp.full((REQ // 2, TOK), LOWEST, F32)

    def docs_event(e):
        k, m = e, (e + 2) % CHUNKS
        docs_up[k].wait_recv()
        if e < CHUNKS // 2:
            span = lat(h_down, k * part, part)
            pass_up[e] = remote(span, span, ys.at[0, 5 + e], yr.at[0, 5 + e], up)
        cross(lat(h_down, k * part, part))
        docs_down[m].wait_recv()
        if e < CHUNKS // 2:
            span = lat(h_up, m * part, part)
            pass_down[e] = remote(span, span, ys.at[1, 5 + e], yr.at[1, 5 + e], down)
        cross(lat(h_up, m * part, part))

    forward(0)
    for copy in weights_in:
        copy.wait()
    own_term()
    advance(1)
    forward(7)
    forward(1)
    take_in(0)
    for copy in passed:
        copy.wait_recv()
    got_table = here(tblx, sm_got, 7)
    own_lat.wait()
    for copy in crossed[0:2]:
        copy.wait_recv()
    turn(y)
    advance(2)
    forward(6)
    forward(2)
    take_in(7)
    take_in(1)
    docs_event(0)
    docs_event(1)
    advance(3)
    forward(5)
    forward(3)
    docs_event(2)
    docs_event(3)
    rope_up.wait_recv()
    span = rope(h_down, 0, DOC_DEV // 2)
    pass_up[2] = remote(span, span, ys.at[0, 7], yr.at[0, 7], up)
    cross(rope(h_down))
    rope_down.wait_recv()
    span = rope(h_up, DOC_DEV // 2, DOC_DEV // 2)
    pass_down[2] = remote(span, span, ys.at[1, 7], yr.at[1, 7], down)
    cross(rope(h_up))
    take_in(6)
    take_in(2)
    for k in range(CHUNKS):
        hops[k * 2 // CHUNKS, 3, k].wait_recv()
    forward(4)
    for copy in crossed[2:12]:
        copy.wait_recv()
    turn((y + 1) % NY)
    turn((y + NY - 1) % NY)
    take_in(5)
    take_in(3)
    for e in range(CHUNKS // 2):
        pass_up[e].wait_recv()
        cross(lat(h_far, e * part, part))
        pass_down[e].wait_recv()
        cross(lat(h_far, (e + 2) * part, part))
    pass_up[2].wait_recv()
    cross(rope(h_far, 0, DOC_DEV // 2))
    pass_down[2].wait_recv()
    cross(rope(h_far, DOC_DEV // 2, DOC_DEV // 2))
    own_table.wait()
    got_table.wait()
    take_in(4)
    for copy in crossed[12:]:
        copy.wait_recv()
    turn((y + 2) % NY)

    attend(4)
    attend(3)
    settle(4, None, [(0, 3, low, pl.ds(0, 1), right), (1, 5, high, pl.ds(1, 1), left)])
    attend(5)
    settle(3, 0, [(2, 2, everything, both, right)])
    attend(2)
    settle(5, 1, [(3, 6, everything, both, left)])
    attend(6)
    settle(2, 2, [(4, 1, everything, both, right)])
    attend(1)
    settle(6, 3, [(5, 7, everything, both, left)])
    attend(7)
    settle(1, 4, [(6, 0, everything, both, right)])
    attend(0)
    settle(7, 5, [(7, 4, everything, both, left)])

    def own_values(head):
        at = head % (HD // HALVES) * VDIM
        return vals[OWN, head // (HD // HALVES), :, :, at : at + VDIM].reshape(TOK, VDIM)

    def last_ready(p):
        falling_v[6, p].wait_recv()
        falling_v[7, p].wait_recv()

    def store(p, at, values):
        first = p * VQ + at
        out_ref[:, first : first + VDIM] = values

    def done(_):
        return None

    falling_l[6].wait_recv()
    falling_l[7].wait_recv()
    merge(
        0, [incoming(0), incoming(4), (own_values, lses[OWN].reshape(REQ, TOK))],
        done, last_ready, store, done,
    )
    for copy in sent:
        copy.wait_send()


def whole(q_nope, q_rope, latent_turned, doc_cache, w_uk, w_uv, doc_slot, doc_blocks, pair_doc, pair_req):
    local = pl.BlockSpec(memory_space=pltpu.VMEM)
    anywhere = pl.BlockSpec(memory_space=pl.ANY)
    scalar = pl.BlockSpec(memory_space=pltpu.SMEM)
    dma = pltpu.SemaphoreType.DMA
    return pl.pallas_call(
        whole_kernel,
        out_shape=jax.ShapeDtypeStruct((TOK, VW), BF16),
        in_specs=[anywhere, anywhere, local, anywhere, anywhere, anywhere] + [scalar] * 4,
        out_specs=local,
        scratch_shapes=[
            pltpu.VMEM((DOC_DEV, NY, 2, 2, POS // 2, RANK), BF16),
            pltpu.VMEM((DOC_DEV, NY, 2, POS // 2, LANES), BF16),
            pltpu.VMEM((DOC_DEV, LATENT, DOC_LEN), BF16),
            pltpu.VMEM((DOC_DEV, 2, POS // 2, LATENT), BF16),
            pltpu.VMEM((HD, NOPE, RANK), BF16),
            pltpu.VMEM((HD, RANK, VDIM), BF16),
            pltpu.VMEM((TOK, LATENT), BF16),
            pltpu.VMEM((NZ, TOK, QW), BF16),
            pltpu.VMEM((NZ, NX, ROWS, QW), BF16),
            pltpu.VMEM((NZ, NX, ROWS, QW), BF16),
            pltpu.VMEM((NZ, 1, TBL), jnp.int32),
            pltpu.VMEM((NZ, 1, TBL), jnp.int32),
            pltpu.VMEM((NX, NZ, 1, TBL), jnp.int32),
            pltpu.SMEM((NZ, 1, TBL), jnp.int32),
            pltpu.SMEM((NX, NZ, 1, TBL), jnp.int32),
            pltpu.VMEM(((NZ + 1) * GROUP, HD, Q_LEN, RANK), BF16),
            pltpu.VMEM(((NZ + 1) * GROUP, HD, Q_LEN, ROPE), BF16),
            pltpu.VMEM((GROUP, HD, Q_LEN, VDIM), F32),
            pltpu.VMEM((NZ + 1, HALVES, NX, ROWS, VW // HALVES), BF16),
            pltpu.VMEM((NZ + 1, NX, CAP, TOK), F32),
            pltpu.VMEM((NZ, HALVES, NX, ROWS, VW // HALVES), BF16),
            pltpu.VMEM((NZ, NX, CAP, TOK), F32),
            pltpu.VMEM((NZ, QUARTERS, TOK, VQ), BF16),
            pltpu.VMEM((NZ, 2, REQ // 2, TOK), F32),
            pltpu.VMEM((NZ, QUARTERS, TOK, VQ), BF16),
            pltpu.VMEM((NZ, 2, REQ // 2, TOK), F32),
            dma((2, 4, CHUNKS)), dma((2, 4, CHUNKS)),
            dma((NZ,)), dma((NZ,)),
            dma((NX,)), dma((NX,)),
            dma((NZ, NX)), dma((NZ, NX)),
            dma((2, 8)), dma((2, 8)),
            dma((18,)), dma((18,)),
            dma((NZ, HALVES, NX)), dma((NZ, HALVES, NX)),
            dma((NZ, NX)), dma((NZ, NX)),
            dma((8, QUARTERS)), dma((8, QUARTERS)),
            dma((8,)), dma((8,)),
            dma((8,)),
        ],
        compiler_params=pltpu.CompilerParams(
            collective_id=0, has_side_effects=True, vmem_limit_bytes=VMEM_LIMIT
        ),
        name="whole",
    )(q_nope, q_rope, latent_turned, doc_cache, w_uk, w_uv, doc_slot, doc_blocks, pair_doc, pair_req)


def on_device(
    q_nope, q_rope, question_latent, doc_cache, w_uk, w_uv, doc_slot, doc_blocks, pair_doc, pair_req
):
    return whole(
        q_nope, q_rope, question_latent.T, doc_cache.reshape(DOC_DEV, 2, POS // 2, LATENT),
        w_uk, w_uv, doc_slot, doc_blocks, pair_doc, pair_req,
    )


def solution(mesh):
    placed = (
        P("doc", "head"),
        P("doc", "head"),
        P("doc", None),
        P("doc", "head", None),
        P("head", None, None),
        P("head", None, None),
        P(),
        P(),
        P("doc"),
        P("doc"),
    )
    return jax.shard_map(
        on_device, mesh=mesh, in_specs=placed, out_specs=P("doc", "head"), check_vma=False
    )
```

```python
import jax
import jax.numpy as jnp
from jax import lax
from jax.experimental import pallas as pl
from jax.experimental.pallas import tpu as pltpu
from jax.sharding import PartitionSpec as P

RANK = 512
ROPE = 64
NOPE = 128
VDIM = 128
LATENT = RANK + ROPE
Q_LEN = 16
BLOCK = 128
DOC_LEN = 512
HD = 8
TOK = 128
REQ = 8
DOC_DEV = 16
PAIRS = 32
CAP = 2
ROWS = CAP * Q_LEN
NX, NZ, NY = 4, 8, 4
N_DOC = NX * NZ
SLOTS = N_DOC * CAP
GROUP = NX * CAP
CHUNKS = 4
HALVES = 2
QUARTERS = 4
VQ = HD * VDIM // QUARTERS
OWN = NZ
NW = HD * NOPE
QW = HD * (NOPE + ROPE)
VW = HD * VDIM
POS = 64
LANES = 128
TBL = 3 * NX * ROWS
SCALE = (NOPE + ROPE) ** (-0.5)
LN2 = 0.6931471805599453
EXP2_SCALE = SCALE / LN2
LOWEST = -1e30
MESH = pl.DeviceIdType.MESH
F32 = jnp.float32
BF16 = jnp.bfloat16
VMEM_LIMIT = 62 * 1024 * 1024


def dot(a, b, dims):
    return lax.dot_general(a, b, (dims, ((), ())), preferred_element_type=F32)


def whole_kernel(
    qn_ref, qr_ref, qlt_ref, doc_ref, uk_hbm, uv_hbm, slot_ref, blocks_ref, name_ref, request_ref, out_ref,
    full_lat, full_rope, kt, doc_in, uk_ref, uv_ref, ql, gq, sendb, slots, tbl, tblb, tblx, sm_own, sm_got,
    qa, q_rope, inv, vals, lses, xv, xl, pv, plse, in_v, in_l,
    zs, zr, ts, tr, us, ur, xs, xr, ys, yr, cs, cr, vs, vr, es, er, ps, pr, fs, fr, ls,
):
    d = lax.axis_index("doc")
    h = lax.axis_index("head")
    z, x = d // NX, d % NX
    y, c = h // 2, h % 2
    z_peer = [None] + [(((z + j) % NZ) * NX + x, h) for j in range(1, NZ)]
    x_peer = [None] + [(z * NX + (x + j) % NX, h) for j in range(1, NX)]
    right, left = z_peer[1], z_peer[NZ - 1]
    h_up = ((y + 1) % NY) * 2 + c
    h_down = ((y + NY - 1) % NY) * 2 + c
    h_far = ((y + 2) % NY) * 2 + c
    up, down, other = (d, h_up), (d, h_down), (d, y * 2 + 1 - c)

    barrier = pltpu.get_barrier_semaphore()
    greeted = z_peer[1:] + x_peer[1:] + [up, down, other]
    for peer in greeted:
        pl.semaphore_signal(barrier, inc=1, device_id=peer, device_id_type=MESH)

    def here(src, dst, i):
        copy = pltpu.make_async_copy(src, dst, ls.at[i])
        copy.start()
        return copy

    doc_lat = doc_ref.at[:, :, :, pl.ds(0, RANK)]

    def lat(head, first=0, count=DOC_DEV):
        return full_lat.at[pl.ds(first, count), head // 2, :, head % 2]

    def rope(head, first=0, count=DOC_DEV):
        return full_rope.at[pl.ds(first, count), head // 2, head % 2]

    queries_in = [
        here(qn_ref, gq.at[0, :, pl.ds(0, NW)], 0),
        here(qr_ref, gq.at[0, :, pl.ds(NW, QW - NW)], 1),
    ]
    docs_in = here(doc_ref, doc_in, 2)
    own_lat = here(doc_lat, lat(h), 3)
    weights_in = [here(uk_hbm, uk_ref, 4), here(uv_hbm, uv_ref, 5)]
    lane = lax.broadcasted_iota(jnp.int32, (NZ, TOK), 1)
    channel = lax.broadcasted_iota(jnp.int32, (NZ, TOK), 0) * NX + lane // ROWS
    turn_at = (lane % ROWS) // Q_LEN
    token_at = lane % Q_LEN

    def route(k, carry):
        tokens, docs, blocks, filled = carry
        name = name_ref[k]
        place = slot_ref[name]
        mine = channel == place // DOC_DEV
        put = mine & (turn_at == filled)
        return (
            jnp.where(put, request_ref[k] * Q_LEN + token_at, tokens),
            jnp.where(put, place % DOC_DEV, docs),
            jnp.where(put, blocks_ref[name], blocks),
            jnp.where(mine, filled + 1, filled),
        )

    nothing = jnp.zeros((NZ, TOK), jnp.int32)
    routed = lax.fori_loop(0, PAIRS, route, (nothing - 1, nothing, nothing, nothing))
    for k in range(3):
        tbl[:, :, k * TOK : (k + 1) * TOK] = routed[k].reshape(NZ, 1, TOK)
    for copy in queries_in:
        copy.wait()
    pl.semaphore_wait(barrier, len(greeted))

    sent = []

    def remote(src, dst, send, recv, peer):
        copy = pltpu.make_async_remote_copy(
            src_ref=src, dst_ref=dst, send_sem=send, recv_sem=recv, device_id=peer, device_id_type=MESH
        )
        copy.start()
        sent.append(copy)
        return copy

    half = TOK // 2
    low, high = pl.ds(0, half), pl.ds(half, half)
    chain = ((0, 7, 6, 5, 4), (0, 1, 2, 3, 4))
    hops = {}

    def hop(way, step, k):
        rows = pl.ds(k * (TOK // CHUNKS), TOK // CHUNKS)
        hops[way, step, k] = remote(
            gq.at[chain[way][step], rows], gq.at[chain[way][step + 1], rows],
            zs.at[way, step, k], zr.at[way, step, k], (right, left)[way],
        )

    for k in range(CHUNKS):
        hop(0, 0, k)
        hop(1, 0, k)

    def advance(step):
        for k in range(CHUNKS):
            for way in range(2):
                hops[way, step - 1, k].wait_recv()
                if step < 3 or (k < CHUNKS // 2) == (way == 0):
                    hop(way, step, k)

    part = DOC_DEV // CHUNKS
    docs_up, docs_down, pass_up, pass_down, crossed = {}, {}, {}, {}, []

    def cross(src):
        i = len(crossed)
        crossed.append(remote(src, src, cs.at[i], cr.at[i], other))

    def doc_part(k):
        return doc_ref.at[pl.ds(k * part, part), :, :, pl.ds(0, RANK)]

    def send_docs(e):
        k, m = e, (e + 2) % CHUNKS
        docs_up[k] = remote(doc_part(k), lat(h, k * part, part), ys.at[0, k], yr.at[0, k], up)
        docs_down[m] = remote(doc_part(m), lat(h, m * part, part), ys.at[1, m], yr.at[1, m], down)

    send_docs(0)
    send_docs(1)
    crossed.append(remote(doc_lat, lat(h), cs.at[0], cr.at[0], other))

    tables = [
        remote(tbl.at[(z + j) % NZ], tblb.at[z], ts.at[j], tr.at[j], z_peer[j]) for j in range(1, NZ)
    ]
    tblb[pl.ds(z, 1)] = tbl[pl.ds(z, 1)]

    docs_in.wait()
    packed = jnp.concatenate([doc_in[:, 0, :, RANK:LATENT], doc_in[:, 1, :, RANK:LATENT]], axis=2)
    full_rope[:, pl.ds(y, 1), pl.ds(c, 1)] = packed.reshape(DOC_DEV, 1, 1, POS // 2, LANES)
    rope_up = remote(rope(h), rope(h), ys.at[0, 4], yr.at[0, 4], up)
    rope_down = remote(rope(h), rope(h), ys.at[1, 4], yr.at[1, 4], down)
    cross(rope(h))

    token = lax.broadcasted_iota(jnp.int32, (TOK, NX * ROWS), 0)
    arriving = {}

    def picked(rel):
        wanted = tblb[(z + rel) % NZ][:, 0:TOK]
        return jnp.where(token == wanted, 1.0, 0.0).astype(BF16)

    def forward(rel):
        pick = picked(rel)
        for k in range(0, QW, 512):
            chosen = dot(pick, gq[rel, :, k : k + 512], ((0,), (0,))).astype(BF16)
            sendb[rel, :, :, k : k + 512] = chosen.reshape(NX, ROWS, 512)
        arriving[rel] = [
            remote(
                sendb.at[rel, (x + j) % NX], slots.at[rel, x], xs.at[rel, j], xr.at[rel, j], x_peer[j]
            )
            for j in range(1, NX)
        ]
        slots[rel, pl.ds(x, 1)] = sendb[rel, pl.ds(x, 1)]

    def absorb(group, rows):
        span = pl.ds(group * GROUP, GROUP)
        for head in range(HD):
            nope = rows(head * NOPE, NOPE).reshape(TOK, NOPE)
            absorbed = dot(nope, uk_ref[head], ((1,), (0,))).astype(BF16)
            qa[span, head] = absorbed.reshape(GROUP, Q_LEN, RANK)
            q_rope[span, head] = rows(NW + head * ROPE, ROPE).reshape(GROUP, Q_LEN, ROPE)

    def take_in(rel):
        for copy in arriving[rel]:
            copy.wait_recv()
        absorb(rel, lambda first, width: slots[rel, :, :, first : first + width])

    row = lax.broadcasted_iota(jnp.int32, (TOK, TOK), 0)
    column = lax.broadcasted_iota(jnp.int32, (TOK, TOK), 1)
    diagonal = row == column

    def softmax(scores):
        largest = jnp.max(scores, axis=1, keepdims=True) * EXP2_SCALE
        weights = jnp.exp2(scores * EXP2_SCALE - largest)
        totals = jnp.sum(weights, axis=1, keepdims=True)
        lse = largest * LN2 + jnp.log(totals)
        as_row = jnp.sum(jnp.where(diagonal, lse, 0.0), axis=0, keepdims=True)
        return weights.astype(BF16), 1.0 / totals, as_row

    def finish(slot, i, weights, scale, keys):
        latent = dot(weights, keys, ((1,), (0,)))
        qa[slot] = latent.astype(BF16).reshape(HD, Q_LEN, RANK)
        inv[i] = jnp.broadcast_to(scale, (TOK, VDIM)).reshape(HD, Q_LEN, VDIM)

    def project(group, part_of):
        for j in range(HD // HALVES):
            head = part_of * (HD // HALVES) + j
            latent = qa[pl.ds(group * GROUP, GROUP), head].reshape(TOK, RANK)
            values = dot(latent, uv_ref[head], ((1,), (0,))) * inv[:, head].reshape(TOK, VDIM)
            vals[group, part_of, :, :, j * VDIM : (j + 1) * VDIM] = values.astype(BF16).reshape(
                NX, ROWS, VDIM
            )

    def own_start():
        for k in range(0, LATENT, LANES):
            width = min(LANES, LATENT - k)
            ql[:, k : k + width] = jnp.transpose(qlt_ref[k : k + width].astype(F32)).astype(BF16)
        absorb(OWN, lambda first, width: gq[0, :, first : first + width])

    def own_part(requests):
        key_at = lax.broadcasted_iota(jnp.int32, (TOK, Q_LEN), 1)
        query_at = lax.broadcasted_iota(jnp.int32, (TOK, Q_LEN), 0) % Q_LEN
        for r in requests:
            slot = OWN * GROUP + r
            keys = ql[r * Q_LEN : (r + 1) * Q_LEN, 0:RANK]
            rope_k = ql[r * Q_LEN : (r + 1) * Q_LEN, RANK:LATENT]
            scores = dot(qa[slot].reshape(TOK, RANK), keys, ((1,), (1,))) + dot(
                q_rope[slot].reshape(TOK, ROPE), rope_k, ((1,), (1,))
            )
            weights, scale, as_row = softmax(jnp.where(key_at <= query_at, scores, LOWEST))
            lses[OWN, r // CAP, r % CAP : r % CAP + 1] = as_row
            finish(slot, r, weights, scale, keys)

    def turn(block, parts=((0, DOC_DEV),)):
        columns = pl.ds(pl.multiple_of(block * BLOCK, BLOCK), BLOCK)

        def one_doc(doc, carry):
            kt[doc, 0:RANK, columns] = jnp.transpose(full_lat[doc, block].reshape(BLOCK, RANK))
            turned = jnp.transpose(full_rope[doc, block].reshape(POS, LANES).astype(F32)).astype(BF16)
            kt[doc, RANK:LATENT, columns] = jnp.concatenate([turned[0:ROPE], turned[ROPE:LANES]], axis=1)
            return carry

        for first, last in parts:
            lax.fori_loop(first, last, one_doc, 0)

    key_block = lax.broadcasted_iota(jnp.int32, (1, DOC_LEN), 1) // BLOCK
    returning = {}

    def attend(rel):
        owner = (z + rel) % NZ
        jobs = []
        for index in range(GROUP):
            source, turn_of = index // CAP, index % CAP
            first = x * ROWS + turn_of * Q_LEN
            doc = sm_got[source, owner, 0, TOK + first]
            blocks = sm_got[source, owner, 0, 2 * TOK + first]
            slot = rel * GROUP + index
            scores = dot(qa[slot].reshape(TOK, RANK), kt[doc, 0:RANK], ((1,), (0,))) + dot(
                q_rope[slot].reshape(TOK, ROPE), kt[doc, RANK:LATENT], ((1,), (0,))
            )
            jobs.append((source, turn_of, doc, blocks, index, slot, scores))
        soft = []
        for source, turn_of, doc, blocks, index, slot, scores in jobs:
            hide = jnp.where(key_block < blocks, 0.0, LOWEST)
            soft.append(softmax(scores + hide))
        for (source, turn_of, doc, blocks, index, slot, scores), (weights, scale, as_row) in zip(jobs, soft):
            lses[rel, source, turn_of : turn_of + 1] = as_row
            finish(slot, index, weights, scale, full_lat[doc].reshape(DOC_LEN, RANK))
        returning[rel] = [
            [
                remote(lses.at[rel, (x + j) % NX], xl.at[rel, x], es.at[rel, j], er.at[rel, j], x_peer[j])
                for j in range(1, NX)
            ]
        ]
        xl[rel, pl.ds(x, 1)] = lses[rel, pl.ds(x, 1)]
        for p in range(HALVES):
            project(rel, p)
            returning[rel].append(
                [
                    remote(
                        vals.at[rel, p, (x + j) % NX], xv.at[rel, p, x],
                        vs.at[rel, p, j], vr.at[rel, p, j], x_peer[j],
                    )
                    for j in range(1, NX)
                ]
            )
            xv[rel, p, pl.ds(x, 1)] = vals[rel, p, pl.ds(x, 1)]

    request_at = lax.broadcasted_iota(jnp.int32, (REQ, TOK), 0) * Q_LEN

    def merge(rel, partials, lse_done, part_ready, store, part_done):
        owner = (z + rel) % NZ
        pick = picked(rel)
        for copy in returning[rel][0]:
            copy.wait_recv()
        hits, rows = [], []
        for s in range(GROUP):
            hits.append(request_at == sm_own[owner, 0, s * Q_LEN])
            rows.append(xl[rel, s // CAP, s % CAP : s % CAP + 1])
        top = jnp.full((REQ, TOK), LOWEST, F32)
        for _, lse in partials:
            top = jnp.maximum(top, lse)
        for hit, lse in zip(hits, rows):
            top = jnp.maximum(top, jnp.where(hit, lse, LOWEST))
        part_share = [jnp.exp(lse - top) for _, lse in partials]
        slot_share = [jnp.where(hit, jnp.exp(lse - top), 0.0) for hit, lse in zip(hits, rows)]
        total = jnp.maximum(sum(part_share + slot_share), 1e-30)
        lse_done(top + jnp.log(total))
        scale = 1.0 / total
        shares = [share * scale for share in part_share] + [
            jnp.sum(share * scale, axis=0, keepdims=True) for share in slot_share
        ]
        turned = jnp.transpose(jnp.concatenate(shares, axis=0))
        count = len(partials)
        for p in range(HALVES):
            for copy in returning[rel][1 + p]:
                copy.wait_recv()
            for j in range(HD // HALVES):
                head = p * (HD // HALVES) + j
                quarter, at_quarter = head // 2, head % 2 * VDIM
                if head % 2 == 0:
                    part_ready(quarter)
                mine = turned[head * Q_LEN : (head + 1) * Q_LEN]

                def stacked(first):
                    return jnp.concatenate([mine[:, k : k + 1] for k in range(first, first + REQ)], axis=0)

                at = j * VDIM
                slot_values = xv[rel, p, :, :, at : at + VDIM].reshape(TOK, VDIM).astype(F32)
                scaled = (slot_values * stacked(count * REQ)).astype(BF16)
                result = dot(pick, scaled, ((1,), (0,)))
                for k, (values, _) in enumerate(partials):
                    result = result + values(head).astype(F32) * stacked(k * REQ)
                store(quarter, at_quarter, result.astype(BF16))
                if head % 2 == 1:
                    part_done(quarter)

    def incoming(i):
        def values(head):
            return in_v[i, head // 2, :, head % 2 * VDIM : (head % 2 + 1) * VDIM]

        return values, in_l[i].reshape(REQ, TOK)

    falling_l, falling_v = {}, {}
    everything, both = pl.ds(0, TOK), pl.ds(0, 2)

    def settle(rel, awaited, moves):
        def lse_done(lse):
            plse[rel] = lse.reshape(2, REQ // 2, TOK)
            for i, target, span, span_l, peer in moves:
                falling_l[i] = remote(
                    plse.at[rel, span_l], in_l.at[target, span_l], fs.at[i], fr.at[i], peer
                )

        def part_ready(p):
            if awaited is not None:
                falling_v[awaited, p].wait_recv()

        def store(p, at, values):
            pv[rel, p, :, at : at + VDIM] = values

        def part_done(p):
            for i, target, span, span_l, peer in moves:
                falling_v[i, p] = remote(
                    pv.at[rel, p, span], in_v.at[target, p, span], ps.at[i, p], pr.at[i, p], peer
                )

        partials = []
        if awaited is not None:
            falling_l[awaited].wait_recv()
            partials = [incoming(rel)]
        merge(rel, partials, lse_done, part_ready, store, part_done)

    in_v[3, :, half:TOK] = jnp.zeros((QUARTERS, half, VQ), BF16)
    in_v[5, :, 0:half] = jnp.zeros((QUARTERS, half, VQ), BF16)
    in_l[3, 1] = jnp.full((REQ // 2, TOK), LOWEST, F32)
    in_l[5, 0] = jnp.full((REQ // 2, TOK), LOWEST, F32)

    def docs_event(e):
        k, m = e, (e + 2) % CHUNKS
        docs_up[k].wait_recv()
        if e < CHUNKS // 2:
            span = lat(h_down, k * part, part)
            pass_up[e] = remote(span, span, ys.at[0, 5 + e], yr.at[0, 5 + e], up)
        cross(lat(h_down, k * part, part))
        docs_down[m].wait_recv()
        if e < CHUNKS // 2:
            span = lat(h_up, m * part, part)
            pass_down[e] = remote(span, span, ys.at[1, 5 + e], yr.at[1, 5 + e], down)
        cross(lat(h_up, m * part, part))

    forward(0)
    for copy in tables:
        copy.wait_recv()
    passed = [remote(tblb, tblx.at[x], us.at[j], ur.at[j], x_peer[j]) for j in range(1, NX)]
    tblx[pl.ds(x, 1)] = tblb[...].reshape(1, NZ, 1, TBL)
    own_table = here(tblb, sm_own, 6)
    send_docs(2)
    send_docs(3)
    for copy in weights_in:
        copy.wait()
    own_start()
    own_part(range(0, REQ // 2))
    own_lat.wait()
    for copy in crossed[0:2]:
        copy.wait_recv()
    turn(y)
    advance(1)
    forward(7)
    forward(1)
    for copy in passed:
        copy.wait_recv()
    got_table = here(tblx, sm_got, 7)
    docs_event(0)
    docs_event(1)
    own_part(range(REQ // 2, REQ))
    for p in range(HALVES):
        project(OWN, p)
    take_in(0)
    advance(2)
    forward(6)
    forward(2)
    rope_up.wait_recv()
    span = rope(h_down, 0, DOC_DEV // 2)
    pass_up[2] = remote(span, span, ys.at[0, 7], yr.at[0, 7], up)
    cross(rope(h_down))
    rope_down.wait_recv()
    span = rope(h_up, DOC_DEV // 2, DOC_DEV // 2)
    pass_down[2] = remote(span, span, ys.at[1, 7], yr.at[1, 7], down)
    cross(rope(h_up))
    take_in(7)
    take_in(1)
    advance(3)
    forward(5)
    forward(3)
    docs_event(2)
    docs_event(3)
    for k in range(CHUNKS):
        hops[k * 2 // CHUNKS, 3, k].wait_recv()
    forward(4)
    take_in(6)
    take_in(2)
    for copy in crossed[2:12]:
        copy.wait_recv()
    turn((y + 1) % NY)
    pass_up[2].wait_recv()
    cross(rope(h_far, 0, DOC_DEV // 2))
    pass_down[2].wait_recv()
    cross(rope(h_far, DOC_DEV // 2, DOC_DEV // 2))
    pass_up[0].wait_recv()
    cross(lat(h_far, 0, part))
    pass_down[0].wait_recv()
    cross(lat(h_far, 2 * part, part))
    turn((y + NY - 1) % NY)
    pass_up[1].wait_recv()
    cross(lat(h_far, part, part))
    pass_down[1].wait_recv()
    cross(lat(h_far, 3 * part, part))
    take_in(5)
    take_in(3)
    own_table.wait()
    got_table.wait()
    for copy in crossed[12:16]:
        copy.wait_recv()
    turn((y + 2) % NY, ((0, part), (2 * part, 3 * part)))
    take_in(4)
    for copy in crossed[16:]:
        copy.wait_recv()
    turn((y + 2) % NY, ((part, 2 * part), (3 * part, 4 * part)))

    attend(4)
    attend(3)
    settle(4, None, [(0, 3, low, pl.ds(0, 1), right), (1, 5, high, pl.ds(1, 1), left)])
    attend(5)
    settle(3, 0, [(2, 2, everything, both, right)])
    attend(2)
    settle(5, 1, [(3, 6, everything, both, left)])
    attend(6)
    settle(2, 2, [(4, 1, everything, both, right)])
    attend(1)
    settle(6, 3, [(5, 7, everything, both, left)])
    attend(7)
    settle(1, 4, [(6, 0, everything, both, right)])
    attend(0)
    settle(7, 5, [(7, 4, everything, both, left)])

    def own_values(head):
        at = head % (HD // HALVES) * VDIM
        return vals[OWN, head // (HD // HALVES), :, :, at : at + VDIM].reshape(TOK, VDIM)

    def last_ready(p):
        falling_v[6, p].wait_recv()
        falling_v[7, p].wait_recv()

    def store(p, at, values):
        first = p * VQ + at
        out_ref[:, first : first + VDIM] = values

    def done(_):
        return None

    falling_l[6].wait_recv()
    falling_l[7].wait_recv()
    merge(
        0, [incoming(0), incoming(4), (own_values, lses[OWN].reshape(REQ, TOK))],
        done, last_ready, store, done,
    )
    for copy in sent:
        copy.wait_send()


def whole(q_nope, q_rope, latent_turned, doc_cache, w_uk, w_uv, doc_slot, doc_blocks, pair_doc, pair_req):
    local = pl.BlockSpec(memory_space=pltpu.VMEM)
    anywhere = pl.BlockSpec(memory_space=pl.ANY)
    scalar = pl.BlockSpec(memory_space=pltpu.SMEM)
    dma = pltpu.SemaphoreType.DMA
    return pl.pallas_call(
        whole_kernel,
        out_shape=jax.ShapeDtypeStruct((TOK, VW), BF16),
        in_specs=[anywhere, anywhere, local, anywhere, anywhere, anywhere] + [scalar] * 4,
        out_specs=local,
        scratch_shapes=[
            pltpu.VMEM((DOC_DEV, NY, 2, 2, POS // 2, RANK), BF16),
            pltpu.VMEM((DOC_DEV, NY, 2, POS // 2, LANES), BF16),
            pltpu.VMEM((DOC_DEV, LATENT, DOC_LEN), BF16),
            pltpu.VMEM((DOC_DEV, 2, POS // 2, LATENT), BF16),
            pltpu.VMEM((HD, NOPE, RANK), BF16),
            pltpu.VMEM((HD, RANK, VDIM), BF16),
            pltpu.VMEM((TOK, LATENT), BF16),
            pltpu.VMEM((NZ, TOK, QW), BF16),
            pltpu.VMEM((NZ, NX, ROWS, QW), BF16),
            pltpu.VMEM((NZ, NX, ROWS, QW), BF16),
            pltpu.VMEM((NZ, 1, TBL), jnp.int32),
            pltpu.VMEM((NZ, 1, TBL), jnp.int32),
            pltpu.VMEM((NX, NZ, 1, TBL), jnp.int32),
            pltpu.SMEM((NZ, 1, TBL), jnp.int32),
            pltpu.SMEM((NX, NZ, 1, TBL), jnp.int32),
            pltpu.VMEM(((NZ + 1) * GROUP, HD, Q_LEN, RANK), BF16),
            pltpu.VMEM(((NZ + 1) * GROUP, HD, Q_LEN, ROPE), BF16),
            pltpu.VMEM((GROUP, HD, Q_LEN, VDIM), F32),
            pltpu.VMEM((NZ + 1, HALVES, NX, ROWS, VW // HALVES), BF16),
            pltpu.VMEM((NZ + 1, NX, CAP, TOK), F32),
            pltpu.VMEM((NZ, HALVES, NX, ROWS, VW // HALVES), BF16),
            pltpu.VMEM((NZ, NX, CAP, TOK), F32),
            pltpu.VMEM((NZ, QUARTERS, TOK, VQ), BF16),
            pltpu.VMEM((NZ, 2, REQ // 2, TOK), F32),
            pltpu.VMEM((NZ, QUARTERS, TOK, VQ), BF16),
            pltpu.VMEM((NZ, 2, REQ // 2, TOK), F32),
            dma((2, 4, CHUNKS)), dma((2, 4, CHUNKS)),
            dma((NZ,)), dma((NZ,)),
            dma((NX,)), dma((NX,)),
            dma((NZ, NX)), dma((NZ, NX)),
            dma((2, 8)), dma((2, 8)),
            dma((18,)), dma((18,)),
            dma((NZ, HALVES, NX)), dma((NZ, HALVES, NX)),
            dma((NZ, NX)), dma((NZ, NX)),
            dma((8, QUARTERS)), dma((8, QUARTERS)),
            dma((8,)), dma((8,)),
            dma((8,)),
        ],
        compiler_params=pltpu.CompilerParams(
            collective_id=0, has_side_effects=True, vmem_limit_bytes=VMEM_LIMIT
        ),
        name="whole",
    )(q_nope, q_rope, latent_turned, doc_cache, w_uk, w_uv, doc_slot, doc_blocks, pair_doc, pair_req)


def on_device(
    q_nope, q_rope, question_latent, doc_cache, w_uk, w_uv, doc_slot, doc_blocks, pair_doc, pair_req
):
    return whole(
        q_nope, q_rope, question_latent.T, doc_cache.reshape(DOC_DEV, 2, POS // 2, LATENT),
        w_uk, w_uv, doc_slot, doc_blocks, pair_doc, pair_req,
    )


def solution(mesh):
    placed = (
        P("doc", "head"),
        P("doc", "head"),
        P("doc", None),
        P("doc", "head", None),
        P("head", None, None),
        P("head", None, None),
        P(),
        P(),
        P("doc"),
        P("doc"),
    )
    return jax.shard_map(
        on_device, mesh=mesh, in_specs=placed, out_specs=P("doc", "head"), check_vma=False
    )
```

```python
import jax
import jax.numpy as jnp
from jax import lax
from jax.experimental import pallas as pl
from jax.experimental.pallas import tpu as pltpu
from jax.sharding import PartitionSpec as P

RANK = 512
ROPE = 64
NOPE = 128
VDIM = 128
LATENT = RANK + ROPE
Q_LEN = 16
BLOCK = 128
DOC_LEN = 512
HD = 8
TOK = 128
REQ = 8
DOC_DEV = 16
PAIRS = 32
CAP = 2
ROWS = CAP * Q_LEN
NX, NZ, NY = 4, 8, 4
N_DOC = NX * NZ
SLOTS = N_DOC * CAP
GROUP = NX * CAP
CHUNKS = 4
HALVES = 2
QUARTERS = 4
VQ = HD * VDIM // QUARTERS
OWN = NZ
NW = HD * NOPE
QW = HD * (NOPE + ROPE)
VW = HD * VDIM
POS = 64
LANES = 128
TBL = 3 * NX * ROWS
SCALE = (NOPE + ROPE) ** (-0.5)
LN2 = 0.6931471805599453
EXP2_SCALE = SCALE / LN2
LOWEST = -1e30
MESH = pl.DeviceIdType.MESH
F32 = jnp.float32
BF16 = jnp.bfloat16
VMEM_LIMIT = 62 * 1024 * 1024


def dot(a, b, dims):
    return lax.dot_general(a, b, (dims, ((), ())), preferred_element_type=F32)


def whole_kernel(
    qn_ref, qr_ref, qlt_ref, doc_ref, uk_hbm, uv_hbm, slot_ref, blocks_ref, name_ref, request_ref, out_ref,
    full_lat, full_rope, kt, doc_in, uk_ref, uv_ref, ql, gq, sendb, slots, tbl, tblb, tblx, sm_own, sm_got,
    qa, q_rope, inv, vals, lses, xv, xl, pv, plse, in_v, in_l,
    zs, zr, ts, tr, us, ur, xs, xr, ys, yr, cs, cr, vs, vr, es, er, ps, pr, fs, fr, ls,
):
    d = lax.axis_index("doc")
    h = lax.axis_index("head")
    z, x = d // NX, d % NX
    y, c = h // 2, h % 2
    z_peer = [None] + [(((z + j) % NZ) * NX + x, h) for j in range(1, NZ)]
    x_peer = [None] + [(z * NX + (x + j) % NX, h) for j in range(1, NX)]
    right, left = z_peer[1], z_peer[NZ - 1]
    h_up = ((y + 1) % NY) * 2 + c
    h_down = ((y + NY - 1) % NY) * 2 + c
    h_far = ((y + 2) % NY) * 2 + c
    up, down, other = (d, h_up), (d, h_down), (d, y * 2 + 1 - c)

    barrier = pltpu.get_barrier_semaphore()
    greeted = z_peer[1:] + x_peer[1:] + [up, down, other]
    for peer in greeted:
        pl.semaphore_signal(barrier, inc=1, device_id=peer, device_id_type=MESH)

    def here(src, dst, i):
        copy = pltpu.make_async_copy(src, dst, ls.at[i])
        copy.start()
        return copy

    doc_lat = doc_ref.at[:, :, :, pl.ds(0, RANK)]

    def lat(head, first=0, count=DOC_DEV):
        return full_lat.at[pl.ds(first, count), head // 2, :, head % 2]

    def rope(head, first=0, count=DOC_DEV):
        return full_rope.at[pl.ds(first, count), head // 2, head % 2]

    queries_in = [
        here(qn_ref, gq.at[0, :, pl.ds(0, NW)], 0),
        here(qr_ref, gq.at[0, :, pl.ds(NW, QW - NW)], 1),
    ]
    docs_in = here(doc_ref, doc_in, 2)
    own_lat = here(doc_lat, lat(h), 3)
    weights_in = [here(uk_hbm, uk_ref, 4), here(uv_hbm, uv_ref, 5)]
    lane = lax.broadcasted_iota(jnp.int32, (NZ, TOK), 1)
    channel = lax.broadcasted_iota(jnp.int32, (NZ, TOK), 0) * NX + lane // ROWS
    turn_at = (lane % ROWS) // Q_LEN
    token_at = lane % Q_LEN

    def route(k, carry):
        tokens, docs, blocks, filled = carry
        name = name_ref[k]
        place = slot_ref[name]
        mine = channel == place // DOC_DEV
        put = mine & (turn_at == filled)
        return (
            jnp.where(put, request_ref[k] * Q_LEN + token_at, tokens),
            jnp.where(put, place % DOC_DEV, docs),
            jnp.where(put, blocks_ref[name], blocks),
            jnp.where(mine, filled + 1, filled),
        )

    nothing = jnp.zeros((NZ, TOK), jnp.int32)
    routed = lax.fori_loop(0, PAIRS, route, (nothing - 1, nothing, nothing, nothing))
    for k in range(3):
        tbl[:, :, k * TOK : (k + 1) * TOK] = routed[k].reshape(NZ, 1, TOK)
    for copy in queries_in:
        copy.wait()
    pl.semaphore_wait(barrier, len(greeted))

    sent = []

    def remote(src, dst, send, recv, peer):
        copy = pltpu.make_async_remote_copy(
            src_ref=src, dst_ref=dst, send_sem=send, recv_sem=recv, device_id=peer, device_id_type=MESH
        )
        copy.start()
        sent.append(copy)
        return copy

    half = TOK // 2
    low, high = pl.ds(0, half), pl.ds(half, half)
    chain = ((0, 7, 6, 5, 4), (0, 1, 2, 3, 4))
    hops = {}

    def hop(way, step, k):
        rows = pl.ds(k * (TOK // CHUNKS), TOK // CHUNKS)
        hops[way, step, k] = remote(
            gq.at[chain[way][step], rows], gq.at[chain[way][step + 1], rows],
            zs.at[way, step, k], zr.at[way, step, k], (right, left)[way],
        )

    for k in range(CHUNKS):
        hop(0, 0, k)
        hop(1, 0, k)

    def advance(step):
        for k in range(CHUNKS):
            for way in range(2):
                hops[way, step - 1, k].wait_recv()
                if step < 3 or (k < CHUNKS // 2) == (way == 0):
                    hop(way, step, k)

    part = DOC_DEV // CHUNKS
    docs_up, docs_down, pass_up, pass_down, crossed = {}, {}, {}, {}, []

    def cross(src):
        i = len(crossed)
        crossed.append(remote(src, src, cs.at[i], cr.at[i], other))

    def doc_part(k):
        return doc_ref.at[pl.ds(k * part, part), :, :, pl.ds(0, RANK)]

    def send_docs(e):
        k, m = e, (e + 2) % CHUNKS
        docs_up[k] = remote(doc_part(k), lat(h, k * part, part), ys.at[0, k], yr.at[0, k], up)
        docs_down[m] = remote(doc_part(m), lat(h, m * part, part), ys.at[1, m], yr.at[1, m], down)

    send_docs(0)
    send_docs(1)
    crossed.append(remote(doc_lat, lat(h), cs.at[0], cr.at[0], other))

    tables = [
        remote(tbl.at[(z + j) % NZ], tblb.at[z], ts.at[j], tr.at[j], z_peer[j]) for j in range(1, NZ)
    ]
    tblb[pl.ds(z, 1)] = tbl[pl.ds(z, 1)]

    docs_in.wait()
    packed = jnp.concatenate([doc_in[:, 0, :, RANK:LATENT], doc_in[:, 1, :, RANK:LATENT]], axis=2)
    full_rope[:, pl.ds(y, 1), pl.ds(c, 1)] = packed.reshape(DOC_DEV, 1, 1, POS // 2, LANES)
    rope_up = remote(rope(h), rope(h), ys.at[0, 4], yr.at[0, 4], up)
    rope_down = remote(rope(h), rope(h), ys.at[1, 4], yr.at[1, 4], down)
    cross(rope(h))

    token = lax.broadcasted_iota(jnp.int32, (TOK, NX * ROWS), 0)
    arriving = {}

    def picked(rel):
        wanted = tblb[(z + rel) % NZ][:, 0:TOK]
        return jnp.where(token == wanted, 1.0, 0.0).astype(BF16)

    def forward(rel):
        pick = picked(rel)
        for k in range(0, QW, 512):
            chosen = dot(pick, gq[rel, :, k : k + 512], ((0,), (0,))).astype(BF16)
            sendb[rel, :, :, k : k + 512] = chosen.reshape(NX, ROWS, 512)
        arriving[rel] = [
            remote(
                sendb.at[rel, (x + j) % NX], slots.at[rel, x], xs.at[rel, j], xr.at[rel, j], x_peer[j]
            )
            for j in range(1, NX)
        ]
        slots[rel, pl.ds(x, 1)] = sendb[rel, pl.ds(x, 1)]

    def absorb(group, rows):
        span = pl.ds(group * GROUP, GROUP)
        for head in range(HD):
            nope = rows(head * NOPE, NOPE).reshape(TOK, NOPE)
            absorbed = dot(nope, uk_ref[head], ((1,), (0,))).astype(BF16)
            qa[span, head] = absorbed.reshape(GROUP, Q_LEN, RANK)
            q_rope[span, head] = rows(NW + head * ROPE, ROPE).reshape(GROUP, Q_LEN, ROPE)

    def take_in(rel):
        for copy in arriving[rel]:
            copy.wait_recv()
        absorb(rel, lambda first, width: slots[rel, :, :, first : first + width])

    row = lax.broadcasted_iota(jnp.int32, (TOK, TOK), 0)
    column = lax.broadcasted_iota(jnp.int32, (TOK, TOK), 1)
    diagonal = row == column

    def softmax(scores):
        largest = jnp.max(scores, axis=1, keepdims=True) * EXP2_SCALE
        weights = jnp.exp2(scores * EXP2_SCALE - largest)
        totals = jnp.sum(weights, axis=1, keepdims=True)
        lse = largest * LN2 + jnp.log(totals)
        as_row = jnp.sum(jnp.where(diagonal, lse, 0.0), axis=0, keepdims=True)
        return weights.astype(BF16), 1.0 / totals, as_row

    def finish(slot, i, weights, scale, keys):
        latent = dot(weights, keys, ((1,), (0,)))
        qa[slot] = latent.astype(BF16).reshape(HD, Q_LEN, RANK)
        inv[i] = jnp.broadcast_to(scale, (TOK, VDIM)).reshape(HD, Q_LEN, VDIM)

    def project(group, part_of):
        for j in range(HD // HALVES):
            head = part_of * (HD // HALVES) + j
            latent = qa[pl.ds(group * GROUP, GROUP), head].reshape(TOK, RANK)
            values = dot(latent, uv_ref[head], ((1,), (0,))) * inv[:, head].reshape(TOK, VDIM)
            vals[group, part_of, :, :, j * VDIM : (j + 1) * VDIM] = values.astype(BF16).reshape(
                NX, ROWS, VDIM
            )

    def own_start():
        for k in range(0, LATENT, LANES):
            width = min(LANES, LATENT - k)
            ql[:, k : k + width] = jnp.transpose(qlt_ref[k : k + width].astype(F32)).astype(BF16)
        absorb(OWN, lambda first, width: gq[0, :, first : first + width])

    def own_part(requests):
        key_at = lax.broadcasted_iota(jnp.int32, (TOK, Q_LEN), 1)
        query_at = lax.broadcasted_iota(jnp.int32, (TOK, Q_LEN), 0) % Q_LEN
        for r in requests:
            slot = OWN * GROUP + r
            keys = ql[r * Q_LEN : (r + 1) * Q_LEN, 0:RANK]
            rope_k = ql[r * Q_LEN : (r + 1) * Q_LEN, RANK:LATENT]
            scores = dot(qa[slot].reshape(TOK, RANK), keys, ((1,), (1,))) + dot(
                q_rope[slot].reshape(TOK, ROPE), rope_k, ((1,), (1,))
            )
            weights, scale, as_row = softmax(jnp.where(key_at <= query_at, scores, LOWEST))
            lses[OWN, r // CAP, r % CAP : r % CAP + 1] = as_row
            finish(slot, r, weights, scale, keys)

    def turn(block, parts=((0, DOC_DEV),)):
        columns = pl.ds(pl.multiple_of(block * BLOCK, BLOCK), BLOCK)

        def one_doc(doc, carry):
            kt[doc, 0:RANK, columns] = jnp.transpose(full_lat[doc, block].reshape(BLOCK, RANK))
            turned = jnp.transpose(full_rope[doc, block].reshape(POS, LANES))
            kt[doc, RANK:LATENT, columns] = jnp.concatenate([turned[0:ROPE], turned[ROPE:LANES]], axis=1)
            return carry

        for first, last in parts:
            lax.fori_loop(first, last, one_doc, 0)

    key_block = lax.broadcasted_iota(jnp.int32, (1, DOC_LEN), 1) // BLOCK
    returning = {}

    def attend(rel):
        owner = (z + rel) % NZ
        jobs = []
        for index in range(GROUP):
            source, turn_of = index // CAP, index % CAP
            first = x * ROWS + turn_of * Q_LEN
            doc = sm_got[source, owner, 0, TOK + first]
            blocks = sm_got[source, owner, 0, 2 * TOK + first]
            slot = rel * GROUP + index
            scores = dot(qa[slot].reshape(TOK, RANK), kt[doc, 0:RANK], ((1,), (0,))) + dot(
                q_rope[slot].reshape(TOK, ROPE), kt[doc, RANK:LATENT], ((1,), (0,))
            )
            jobs.append((source, turn_of, doc, blocks, index, slot, scores))
        soft = []
        for source, turn_of, doc, blocks, index, slot, scores in jobs:
            hide = jnp.where(key_block < blocks, 0.0, LOWEST)
            soft.append(softmax(scores + hide))
        for (source, turn_of, doc, blocks, index, slot, scores), (weights, scale, as_row) in zip(jobs, soft):
            lses[rel, source, turn_of : turn_of + 1] = as_row
            finish(slot, index, weights, scale, full_lat[doc].reshape(DOC_LEN, RANK))
        returning[rel] = [
            [
                remote(lses.at[rel, (x + j) % NX], xl.at[rel, x], es.at[rel, j], er.at[rel, j], x_peer[j])
                for j in range(1, NX)
            ]
        ]
        xl[rel, pl.ds(x, 1)] = lses[rel, pl.ds(x, 1)]
        for p in range(HALVES):
            project(rel, p)
            returning[rel].append(
                [
                    remote(
                        vals.at[rel, p, (x + j) % NX], xv.at[rel, p, x],
                        vs.at[rel, p, j], vr.at[rel, p, j], x_peer[j],
                    )
                    for j in range(1, NX)
                ]
            )
            xv[rel, p, pl.ds(x, 1)] = vals[rel, p, pl.ds(x, 1)]

    request_at = lax.broadcasted_iota(jnp.int32, (REQ, TOK), 0) * Q_LEN

    def merge(rel, partials, lse_done, part_ready, store, part_done):
        owner = (z + rel) % NZ
        pick = picked(rel)
        for copy in returning[rel][0]:
            copy.wait_recv()
        hits, rows = [], []
        for s in range(GROUP):
            hits.append(request_at == sm_own[owner, 0, s * Q_LEN])
            rows.append(xl[rel, s // CAP, s % CAP : s % CAP + 1])
        top = jnp.full((REQ, TOK), LOWEST, F32)
        for _, lse in partials:
            top = jnp.maximum(top, lse)
        for hit, lse in zip(hits, rows):
            top = jnp.maximum(top, jnp.where(hit, lse, LOWEST))
        part_share = [jnp.exp(lse - top) for _, lse in partials]
        slot_share = [jnp.where(hit, jnp.exp(lse - top), 0.0) for hit, lse in zip(hits, rows)]
        total = jnp.maximum(sum(part_share + slot_share), 1e-30)
        lse_done(top + jnp.log(total))
        scale = 1.0 / total
        shares = [share * scale for share in part_share] + [
            jnp.sum(share * scale, axis=0, keepdims=True) for share in slot_share
        ]
        turned = jnp.transpose(jnp.concatenate(shares, axis=0))
        count = len(partials)
        for p in range(HALVES):
            for copy in returning[rel][1 + p]:
                copy.wait_recv()
            for j in range(HD // HALVES):
                head = p * (HD // HALVES) + j
                quarter, at_quarter = head // 2, head % 2 * VDIM
                if head % 2 == 0:
                    part_ready(quarter)
                mine = turned[head * Q_LEN : (head + 1) * Q_LEN]

                def stacked(first):
                    return jnp.concatenate([mine[:, k : k + 1] for k in range(first, first + REQ)], axis=0)

                at = j * VDIM
                slot_values = xv[rel, p, :, :, at : at + VDIM].reshape(TOK, VDIM).astype(F32)
                scaled = (slot_values * stacked(count * REQ)).astype(BF16)
                result = dot(pick, scaled, ((1,), (0,)))
                for k, (values, _) in enumerate(partials):
                    result = result + values(head).astype(F32) * stacked(k * REQ)
                store(quarter, at_quarter, result.astype(BF16))
                if head % 2 == 1:
                    part_done(quarter)

    def incoming(i):
        def values(head):
            return in_v[i, head // 2, :, head % 2 * VDIM : (head % 2 + 1) * VDIM]

        return values, in_l[i].reshape(REQ, TOK)

    falling_l, falling_v = {}, {}
    everything, both = pl.ds(0, TOK), pl.ds(0, 2)

    def settle(rel, awaited, moves):
        def lse_done(lse):
            plse[rel] = lse.reshape(2, REQ // 2, TOK)
            for i, target, span, span_l, peer in moves:
                falling_l[i] = remote(
                    plse.at[rel, span_l], in_l.at[target, span_l], fs.at[i], fr.at[i], peer
                )

        def part_ready(p):
            if awaited is not None:
                falling_v[awaited, p].wait_recv()

        def store(p, at, values):
            pv[rel, p, :, at : at + VDIM] = values

        def part_done(p):
            for i, target, span, span_l, peer in moves:
                falling_v[i, p] = remote(
                    pv.at[rel, p, span], in_v.at[target, p, span], ps.at[i, p], pr.at[i, p], peer
                )

        partials = []
        if awaited is not None:
            falling_l[awaited].wait_recv()
            partials = [incoming(rel)]
        merge(rel, partials, lse_done, part_ready, store, part_done)

    in_v[3, :, half:TOK] = jnp.zeros((QUARTERS, half, VQ), BF16)
    in_v[5, :, 0:half] = jnp.zeros((QUARTERS, half, VQ), BF16)
    in_l[3, 1] = jnp.full((REQ // 2, TOK), LOWEST, F32)
    in_l[5, 0] = jnp.full((REQ // 2, TOK), LOWEST, F32)

    def docs_event(e):
        k, m = e, (e + 2) % CHUNKS
        docs_up[k].wait_recv()
        if e < CHUNKS // 2:
            span = lat(h_down, k * part, part)
            pass_up[e] = remote(span, span, ys.at[0, 5 + e], yr.at[0, 5 + e], up)
        cross(lat(h_down, k * part, part))
        docs_down[m].wait_recv()
        if e < CHUNKS // 2:
            span = lat(h_up, m * part, part)
            pass_down[e] = remote(span, span, ys.at[1, 5 + e], yr.at[1, 5 + e], down)
        cross(lat(h_up, m * part, part))

    forward(0)
    for copy in tables:
        copy.wait_recv()
    passed = [remote(tblb, tblx.at[x], us.at[j], ur.at[j], x_peer[j]) for j in range(1, NX)]
    tblx[pl.ds(x, 1)] = tblb[...].reshape(1, NZ, 1, TBL)
    own_table = here(tblb, sm_own, 6)
    send_docs(2)
    send_docs(3)
    for copy in weights_in:
        copy.wait()
    own_start()
    own_lat.wait()
    for copy in crossed[0:2]:
        copy.wait_recv()
    turn(y)
    advance(1)
    forward(7)
    forward(1)
    for copy in passed:
        copy.wait_recv()
    got_table = here(tblx, sm_got, 7)
    docs_event(0)
    docs_event(1)
    take_in(0)
    advance(2)
    forward(6)
    forward(2)
    rope_up.wait_recv()
    span = rope(h_down, 0, DOC_DEV // 2)
    pass_up[2] = remote(span, span, ys.at[0, 7], yr.at[0, 7], up)
    cross(rope(h_down))
    rope_down.wait_recv()
    span = rope(h_up, DOC_DEV // 2, DOC_DEV // 2)
    pass_down[2] = remote(span, span, ys.at[1, 7], yr.at[1, 7], down)
    cross(rope(h_up))
    take_in(7)
    take_in(1)
    advance(3)
    forward(5)
    forward(3)
    docs_event(2)
    docs_event(3)
    for k in range(CHUNKS):
        hops[k * 2 // CHUNKS, 3, k].wait_recv()
    forward(4)
    take_in(6)
    take_in(2)
    for copy in crossed[2:12]:
        copy.wait_recv()
    turn((y + 1) % NY)
    pass_up[2].wait_recv()
    cross(rope(h_far, 0, DOC_DEV // 2))
    pass_down[2].wait_recv()
    cross(rope(h_far, DOC_DEV // 2, DOC_DEV // 2))
    pass_up[0].wait_recv()
    cross(lat(h_far, 0, part))
    pass_down[0].wait_recv()
    cross(lat(h_far, 2 * part, part))
    turn((y + NY - 1) % NY)
    pass_up[1].wait_recv()
    cross(lat(h_far, part, part))
    pass_down[1].wait_recv()
    cross(lat(h_far, 3 * part, part))
    take_in(5)
    take_in(3)
    own_table.wait()
    got_table.wait()
    for copy in crossed[12:16]:
        copy.wait_recv()
    turn((y + 2) % NY, ((0, part), (2 * part, 3 * part)))
    take_in(4)
    for copy in crossed[16:]:
        copy.wait_recv()
    turn((y + 2) % NY, ((part, 2 * part), (3 * part, 4 * part)))

    attend(4)
    attend(3)
    own_part(range(0, REQ))
    for p in range(HALVES):
        project(OWN, p)
    settle(4, None, [(0, 3, low, pl.ds(0, 1), right), (1, 5, high, pl.ds(1, 1), left)])
    attend(5)
    attend(2)
    settle(3, 0, [(2, 2, everything, both, right)])
    attend(6)
    settle(5, 1, [(3, 6, everything, both, left)])
    attend(1)
    settle(2, 2, [(4, 1, everything, both, right)])
    attend(7)
    settle(6, 3, [(5, 7, everything, both, left)])
    attend(0)
    settle(1, 4, [(6, 0, everything, both, right)])
    settle(7, 5, [(7, 4, everything, both, left)])

    def own_values(head):
        at = head % (HD // HALVES) * VDIM
        return vals[OWN, head // (HD // HALVES), :, :, at : at + VDIM].reshape(TOK, VDIM)

    def last_ready(p):
        falling_v[6, p].wait_recv()
        falling_v[7, p].wait_recv()

    def store(p, at, values):
        first = p * VQ + at
        out_ref[:, first : first + VDIM] = values

    def done(_):
        return None

    falling_l[6].wait_recv()
    falling_l[7].wait_recv()
    merge(
        0, [incoming(0), incoming(4), (own_values, lses[OWN].reshape(REQ, TOK))],
        done, last_ready, store, done,
    )
    for copy in sent:
        copy.wait_send()


def whole(q_nope, q_rope, latent_turned, doc_cache, w_uk, w_uv, doc_slot, doc_blocks, pair_doc, pair_req):
    local = pl.BlockSpec(memory_space=pltpu.VMEM)
    anywhere = pl.BlockSpec(memory_space=pl.ANY)
    scalar = pl.BlockSpec(memory_space=pltpu.SMEM)
    dma = pltpu.SemaphoreType.DMA
    return pl.pallas_call(
        whole_kernel,
        out_shape=jax.ShapeDtypeStruct((TOK, VW), BF16),
        in_specs=[anywhere, anywhere, local, anywhere, anywhere, anywhere] + [scalar] * 4,
        out_specs=local,
        scratch_shapes=[
            pltpu.VMEM((DOC_DEV, NY, 2, 2, POS // 2, RANK), BF16),
            pltpu.VMEM((DOC_DEV, NY, 2, POS // 2, LANES), BF16),
            pltpu.VMEM((DOC_DEV, LATENT, DOC_LEN), BF16),
            pltpu.VMEM((DOC_DEV, 2, POS // 2, LATENT), BF16),
            pltpu.VMEM((HD, NOPE, RANK), BF16),
            pltpu.VMEM((HD, RANK, VDIM), BF16),
            pltpu.VMEM((TOK, LATENT), BF16),
            pltpu.VMEM((NZ, TOK, QW), BF16),
            pltpu.VMEM((NZ, NX, ROWS, QW), BF16),
            pltpu.VMEM((NZ, NX, ROWS, QW), BF16),
            pltpu.VMEM((NZ, 1, TBL), jnp.int32),
            pltpu.VMEM((NZ, 1, TBL), jnp.int32),
            pltpu.VMEM((NX, NZ, 1, TBL), jnp.int32),
            pltpu.SMEM((NZ, 1, TBL), jnp.int32),
            pltpu.SMEM((NX, NZ, 1, TBL), jnp.int32),
            pltpu.VMEM(((NZ + 1) * GROUP, HD, Q_LEN, RANK), BF16),
            pltpu.VMEM(((NZ + 1) * GROUP, HD, Q_LEN, ROPE), BF16),
            pltpu.VMEM((GROUP, HD, Q_LEN, VDIM), F32),
            pltpu.VMEM((NZ + 1, HALVES, NX, ROWS, VW // HALVES), BF16),
            pltpu.VMEM((NZ + 1, NX, CAP, TOK), F32),
            pltpu.VMEM((NZ, HALVES, NX, ROWS, VW // HALVES), BF16),
            pltpu.VMEM((NZ, NX, CAP, TOK), F32),
            pltpu.VMEM((NZ, QUARTERS, TOK, VQ), BF16),
            pltpu.VMEM((NZ, 2, REQ // 2, TOK), F32),
            pltpu.VMEM((NZ, QUARTERS, TOK, VQ), BF16),
            pltpu.VMEM((NZ, 2, REQ // 2, TOK), F32),
            dma((2, 4, CHUNKS)), dma((2, 4, CHUNKS)),
            dma((NZ,)), dma((NZ,)),
            dma((NX,)), dma((NX,)),
            dma((NZ, NX)), dma((NZ, NX)),
            dma((2, 8)), dma((2, 8)),
            dma((18,)), dma((18,)),
            dma((NZ, HALVES, NX)), dma((NZ, HALVES, NX)),
            dma((NZ, NX)), dma((NZ, NX)),
            dma((8, QUARTERS)), dma((8, QUARTERS)),
            dma((8,)), dma((8,)),
            dma((8,)),
        ],
        compiler_params=pltpu.CompilerParams(
            collective_id=0, has_side_effects=True, vmem_limit_bytes=VMEM_LIMIT
        ),
        name="whole",
    )(q_nope, q_rope, latent_turned, doc_cache, w_uk, w_uv, doc_slot, doc_blocks, pair_doc, pair_req)


def on_device(
    q_nope, q_rope, question_latent, doc_cache, w_uk, w_uv, doc_slot, doc_blocks, pair_doc, pair_req
):
    return whole(
        q_nope, q_rope, question_latent.T, doc_cache.reshape(DOC_DEV, 2, POS // 2, LATENT),
        w_uk, w_uv, doc_slot, doc_blocks, pair_doc, pair_req,
    )


def solution(mesh):
    placed = (
        P("doc", "head"),
        P("doc", "head"),
        P("doc", None),
        P("doc", "head", None),
        P("head", None, None),
        P("head", None, None),
        P(),
        P(),
        P("doc"),
        P("doc"),
    )
    return jax.shard_map(
        on_device, mesh=mesh, in_specs=placed, out_specs=P("doc", "head"), check_vma=False
    )
```

```python
import jax
import jax.numpy as jnp
from jax import lax
from jax.experimental import pallas as pl
from jax.experimental.pallas import tpu as pltpu
from jax.sharding import PartitionSpec as P

RANK = 512
ROPE = 64
NOPE = 128
VDIM = 128
LATENT = RANK + ROPE
Q_LEN = 16
BLOCK = 128
DOC_LEN = 512
HD = 8
TOK = 128
REQ = 8
DOC_DEV = 16
PAIRS = 32
CAP = 2
ROWS = CAP * Q_LEN
NX, NZ, NY = 4, 8, 4
N_DOC = NX * NZ
SLOTS = N_DOC * CAP
GROUP = NX * CAP
CHUNKS = 4
HALVES = 2
QUARTERS = 4
VQ = HD * VDIM // QUARTERS
OWN = NZ
NW = HD * NOPE
QW = HD * (NOPE + ROPE)
VW = HD * VDIM
POS = 64
LANES = 128
TBL = 3 * NX * ROWS
SCALE = (NOPE + ROPE) ** (-0.5)
LN2 = 0.6931471805599453
EXP2_SCALE = SCALE / LN2
LOWEST = -1e30
MESH = pl.DeviceIdType.MESH
F32 = jnp.float32
BF16 = jnp.bfloat16
VMEM_LIMIT = 62 * 1024 * 1024


def dot(a, b, dims):
    return lax.dot_general(a, b, (dims, ((), ())), preferred_element_type=F32)


def whole_kernel(
    qn_ref, qr_ref, qlt_ref, doc_ref, uk_hbm, uv_hbm, slot_ref, blocks_ref, name_ref, request_ref, out_ref,
    full_lat, full_rope, kt, doc_in, uk_ref, uv_ref, ql, gq, sendb, slots, tbl, tblb, tblx, sm_own, sm_got,
    qa, q_rope, inv, vals, lses, xv, xl, pv, plse, in_v, in_l,
    zs, zr, ts, tr, us, ur, xs, xr, ys, yr, cs, cr, vs, vr, es, er, ps, pr, fs, fr, ls,
):
    d = lax.axis_index("doc")
    h = lax.axis_index("head")
    z, x = d // NX, d % NX
    y, c = h // 2, h % 2
    z_peer = [None] + [(((z + j) % NZ) * NX + x, h) for j in range(1, NZ)]
    x_peer = [None] + [(z * NX + (x + j) % NX, h) for j in range(1, NX)]
    right, left = z_peer[1], z_peer[NZ - 1]
    h_up = ((y + 1) % NY) * 2 + c
    h_down = ((y + NY - 1) % NY) * 2 + c
    h_far = ((y + 2) % NY) * 2 + c
    up, down, other = (d, h_up), (d, h_down), (d, y * 2 + 1 - c)

    barrier = pltpu.get_barrier_semaphore()
    greeted = z_peer[1:] + x_peer[1:] + [up, down, other]
    for peer in greeted:
        pl.semaphore_signal(barrier, inc=1, device_id=peer, device_id_type=MESH)

    def here(src, dst, i):
        copy = pltpu.make_async_copy(src, dst, ls.at[i])
        copy.start()
        return copy

    doc_lat = doc_ref.at[:, :, :, pl.ds(0, RANK)]

    def lat(head, first=0, count=DOC_DEV):
        return full_lat.at[pl.ds(first, count), head // 2, :, head % 2]

    def rope(head, first=0, count=DOC_DEV):
        return full_rope.at[pl.ds(first, count), head // 2, head % 2]

    queries_in = [
        here(qn_ref, gq.at[0, :, pl.ds(0, NW)], 0),
        here(qr_ref, gq.at[0, :, pl.ds(NW, QW - NW)], 1),
    ]
    docs_in = here(doc_ref, doc_in, 2)
    own_lat = here(doc_lat, lat(h), 3)
    weights_in = [here(uk_hbm, uk_ref, 4), here(uv_hbm, uv_ref, 5)]
    lane = lax.broadcasted_iota(jnp.int32, (NZ, TOK), 1)
    channel = lax.broadcasted_iota(jnp.int32, (NZ, TOK), 0) * NX + lane // ROWS
    turn_at = (lane % ROWS) // Q_LEN
    token_at = lane % Q_LEN

    def route(k, carry):
        tokens, docs, blocks, filled = carry
        name = name_ref[k]
        place = slot_ref[name]
        mine = channel == place // DOC_DEV
        put = mine & (turn_at == filled)
        return (
            jnp.where(put, request_ref[k] * Q_LEN + token_at, tokens),
            jnp.where(put, place % DOC_DEV, docs),
            jnp.where(put, blocks_ref[name], blocks),
            jnp.where(mine, filled + 1, filled),
        )

    nothing = jnp.zeros((NZ, TOK), jnp.int32)
    routed = lax.fori_loop(0, PAIRS, route, (nothing - 1, nothing, nothing, nothing))
    for k in range(3):
        tbl[:, :, k * TOK : (k + 1) * TOK] = routed[k].reshape(NZ, 1, TOK)
    for copy in queries_in:
        copy.wait()
    pl.semaphore_wait(barrier, len(greeted))

    sent = []

    def remote(src, dst, send, recv, peer):
        copy = pltpu.make_async_remote_copy(
            src_ref=src, dst_ref=dst, send_sem=send, recv_sem=recv, device_id=peer, device_id_type=MESH
        )
        copy.start()
        sent.append(copy)
        return copy

    half = TOK // 2
    low, high = pl.ds(0, half), pl.ds(half, half)
    chain = ((0, 7, 6, 5, 4), (0, 1, 2, 3, 4))
    hops = {}

    def hop(way, step, k):
        rows = pl.ds(k * (TOK // CHUNKS), TOK // CHUNKS)
        hops[way, step, k] = remote(
            gq.at[chain[way][step], rows], gq.at[chain[way][step + 1], rows],
            zs.at[way, step, k], zr.at[way, step, k], (right, left)[way],
        )

    for k in range(CHUNKS):
        hop(0, 0, k)
        hop(1, 0, k)

    def advance(step):
        for k in range(CHUNKS):
            for way in range(2):
                hops[way, step - 1, k].wait_recv()
                if step < 3 or (k < CHUNKS // 2) == (way == 0):
                    hop(way, step, k)

    part = DOC_DEV // CHUNKS
    docs_up, docs_down, pass_up, pass_down, crossed = {}, {}, {}, {}, []

    def cross(src):
        i = len(crossed)
        crossed.append(remote(src, src, cs.at[i], cr.at[i], other))

    def doc_part(k):
        return doc_ref.at[pl.ds(k * part, part), :, :, pl.ds(0, RANK)]

    def send_docs(e):
        k, m = e, (e + 2) % CHUNKS
        docs_up[k] = remote(doc_part(k), lat(h, k * part, part), ys.at[0, k], yr.at[0, k], up)
        docs_down[m] = remote(doc_part(m), lat(h, m * part, part), ys.at[1, m], yr.at[1, m], down)

    send_docs(0)
    send_docs(1)
    crossed.append(remote(doc_lat, lat(h), cs.at[0], cr.at[0], other))

    tables = [
        remote(tbl.at[(z + j) % NZ], tblb.at[z], ts.at[j], tr.at[j], z_peer[j]) for j in range(1, NZ)
    ]
    tblb[pl.ds(z, 1)] = tbl[pl.ds(z, 1)]

    docs_in.wait()
    packed = jnp.concatenate([doc_in[:, 0, :, RANK:LATENT], doc_in[:, 1, :, RANK:LATENT]], axis=2)
    full_rope[:, pl.ds(y, 1), pl.ds(c, 1)] = packed.reshape(DOC_DEV, 1, 1, POS // 2, LANES)
    rope_up = remote(rope(h), rope(h), ys.at[0, 4], yr.at[0, 4], up)
    rope_down = remote(rope(h), rope(h), ys.at[1, 4], yr.at[1, 4], down)
    cross(rope(h))

    token = lax.broadcasted_iota(jnp.int32, (TOK, NX * ROWS), 0)
    arriving = {}

    def picked(rel):
        wanted = tblb[(z + rel) % NZ][:, 0:TOK]
        return jnp.where(token == wanted, 1.0, 0.0).astype(BF16)

    def forward(rel):
        pick = picked(rel)
        for k in range(0, QW, 512):
            chosen = dot(pick, gq[rel, :, k : k + 512], ((0,), (0,))).astype(BF16)
            sendb[rel, :, :, k : k + 512] = chosen.reshape(NX, ROWS, 512)
        arriving[rel] = [
            remote(
                sendb.at[rel, (x + j) % NX], slots.at[rel, x], xs.at[rel, j], xr.at[rel, j], x_peer[j]
            )
            for j in range(1, NX)
        ]
        slots[rel, pl.ds(x, 1)] = sendb[rel, pl.ds(x, 1)]

    def absorb(group, rows):
        span = pl.ds(group * GROUP, GROUP)
        for head in range(HD):
            nope = rows(head * NOPE, NOPE).reshape(TOK, NOPE)
            absorbed = dot(nope, uk_ref[head], ((1,), (0,))).astype(BF16)
            qa[span, head] = absorbed.reshape(GROUP, Q_LEN, RANK)
            q_rope[span, head] = rows(NW + head * ROPE, ROPE).reshape(GROUP, Q_LEN, ROPE)

    def take_in(rel):
        for copy in arriving[rel]:
            copy.wait_recv()
        absorb(rel, lambda first, width: slots[rel, :, :, first : first + width])

    row = lax.broadcasted_iota(jnp.int32, (TOK, TOK), 0)
    column = lax.broadcasted_iota(jnp.int32, (TOK, TOK), 1)
    diagonal = row == column

    def softmax(scores):
        largest = jnp.max(scores, axis=1, keepdims=True) * EXP2_SCALE
        weights = jnp.exp2(scores * EXP2_SCALE - largest)
        totals = jnp.sum(weights, axis=1, keepdims=True)
        lse = largest * LN2 + jnp.log(totals)
        as_row = jnp.sum(jnp.where(diagonal, lse, 0.0), axis=0, keepdims=True)
        return weights.astype(BF16), 1.0 / totals, as_row

    def finish(slot, i, weights, scale, keys):
        latent = dot(weights, keys, ((1,), (0,)))
        qa[slot] = latent.astype(BF16).reshape(HD, Q_LEN, RANK)
        inv[i] = jnp.broadcast_to(scale, (TOK, VDIM)).reshape(HD, Q_LEN, VDIM)

    def project(group, part_of):
        for j in range(HD // HALVES):
            head = part_of * (HD // HALVES) + j
            latent = qa[pl.ds(group * GROUP, GROUP), head].reshape(TOK, RANK)
            values = dot(latent, uv_ref[head], ((1,), (0,))) * inv[:, head].reshape(TOK, VDIM)
            vals[group, part_of, :, :, j * VDIM : (j + 1) * VDIM] = values.astype(BF16).reshape(
                NX, ROWS, VDIM
            )

    def own_start():
        for k in range(0, LATENT, LANES):
            width = min(LANES, LATENT - k)
            ql[:, k : k + width] = jnp.transpose(qlt_ref[k : k + width].astype(F32)).astype(BF16)
        absorb(OWN, lambda first, width: gq[0, :, first : first + width])

    def own_part(requests):
        key_at = lax.broadcasted_iota(jnp.int32, (TOK, Q_LEN), 1)
        query_at = lax.broadcasted_iota(jnp.int32, (TOK, Q_LEN), 0) % Q_LEN
        for r in requests:
            slot = OWN * GROUP + r
            keys = ql[r * Q_LEN : (r + 1) * Q_LEN, 0:RANK]
            rope_k = ql[r * Q_LEN : (r + 1) * Q_LEN, RANK:LATENT]
            scores = dot(qa[slot].reshape(TOK, RANK), keys, ((1,), (1,))) + dot(
                q_rope[slot].reshape(TOK, ROPE), rope_k, ((1,), (1,))
            )
            weights, scale, as_row = softmax(jnp.where(key_at <= query_at, scores, LOWEST))
            lses[OWN, r // CAP, r % CAP : r % CAP + 1] = as_row
            finish(slot, r, weights, scale, keys)

    def turn(block, parts=((0, DOC_DEV),)):
        columns = pl.ds(pl.multiple_of(block * BLOCK, BLOCK), BLOCK)

        def one_doc(doc, carry):
            kt[doc, 0:RANK, columns] = jnp.transpose(full_lat[doc, block].reshape(BLOCK, RANK))
            turned = jnp.transpose(full_rope[doc, block].reshape(POS, LANES))
            kt[doc, RANK:LATENT, columns] = jnp.concatenate([turned[0:ROPE], turned[ROPE:LANES]], axis=1)
            return carry

        for first, last in parts:
            lax.fori_loop(first, last, one_doc, 0)

    key_block = lax.broadcasted_iota(jnp.int32, (1, DOC_LEN), 1) // BLOCK
    returning = {}

    def attend(rel):
        owner = (z + rel) % NZ
        jobs = []
        for index in range(GROUP):
            source, turn_of = index // CAP, index % CAP
            first = x * ROWS + turn_of * Q_LEN
            doc = sm_got[source, owner, 0, TOK + first]
            blocks = sm_got[source, owner, 0, 2 * TOK + first]
            slot = rel * GROUP + index
            scores = dot(qa[slot].reshape(TOK, RANK), kt[doc, 0:RANK], ((1,), (0,))) + dot(
                q_rope[slot].reshape(TOK, ROPE), kt[doc, RANK:LATENT], ((1,), (0,))
            )
            jobs.append((source, turn_of, doc, blocks, index, slot, scores))
        soft = []
        for source, turn_of, doc, blocks, index, slot, scores in jobs:
            hide = jnp.where(key_block < blocks, 0.0, LOWEST)
            soft.append(softmax(scores + hide))
        for (source, turn_of, doc, blocks, index, slot, scores), (weights, scale, as_row) in zip(jobs, soft):
            lses[rel, source, turn_of : turn_of + 1] = as_row
            finish(slot, index, weights, scale, full_lat[doc].reshape(DOC_LEN, RANK))
        returning[rel] = [
            [
                remote(lses.at[rel, (x + j) % NX], xl.at[rel, x], es.at[rel, j], er.at[rel, j], x_peer[j])
                for j in range(1, NX)
            ]
        ]
        xl[rel, pl.ds(x, 1)] = lses[rel, pl.ds(x, 1)]
        for p in range(HALVES):
            project(rel, p)
            returning[rel].append(
                [
                    remote(
                        vals.at[rel, p, (x + j) % NX], xv.at[rel, p, x],
                        vs.at[rel, p, j], vr.at[rel, p, j], x_peer[j],
                    )
                    for j in range(1, NX)
                ]
            )
            xv[rel, p, pl.ds(x, 1)] = vals[rel, p, pl.ds(x, 1)]

    request_at = lax.broadcasted_iota(jnp.int32, (REQ, TOK), 0) * Q_LEN

    def merge(rel, partials, lse_done, part_ready, store, part_done):
        owner = (z + rel) % NZ
        pick = picked(rel)
        for copy in returning[rel][0]:
            copy.wait_recv()
        hits, rows = [], []
        for s in range(GROUP):
            hits.append(request_at == sm_own[owner, 0, s * Q_LEN])
            rows.append(xl[rel, s // CAP, s % CAP : s % CAP + 1])
        top = jnp.full((REQ, TOK), LOWEST, F32)
        for _, lse in partials:
            top = jnp.maximum(top, lse)
        for hit, lse in zip(hits, rows):
            top = jnp.maximum(top, jnp.where(hit, lse, LOWEST))
        part_share = [jnp.exp(lse - top) for _, lse in partials]
        slot_share = [jnp.where(hit, jnp.exp(lse - top), 0.0) for hit, lse in zip(hits, rows)]
        total = jnp.maximum(sum(part_share + slot_share), 1e-30)
        lse_done(top + jnp.log(total))
        scale = 1.0 / total
        shares = [share * scale for share in part_share] + [
            jnp.sum(share * scale, axis=0, keepdims=True) for share in slot_share
        ]
        turned = jnp.transpose(jnp.concatenate(shares, axis=0))
        count = len(partials)
        for p in range(HALVES):
            for copy in returning[rel][1 + p]:
                copy.wait_recv()
            for j in range(HD // HALVES):
                head = p * (HD // HALVES) + j
                quarter, at_quarter = head // 2, head % 2 * VDIM
                if head % 2 == 0:
                    part_ready(quarter)
                mine = turned[head * Q_LEN : (head + 1) * Q_LEN]

                def stacked(first):
                    return jnp.concatenate([mine[:, k : k + 1] for k in range(first, first + REQ)], axis=0)

                at = j * VDIM
                slot_values = xv[rel, p, :, :, at : at + VDIM].reshape(TOK, VDIM).astype(F32)
                scaled = (slot_values * stacked(count * REQ)).astype(BF16)
                result = dot(pick, scaled, ((1,), (0,)))
                for k, (values, _) in enumerate(partials):
                    result = result + values(head).astype(F32) * stacked(k * REQ)
                store(quarter, at_quarter, result.astype(BF16))
                if head % 2 == 1:
                    part_done(quarter)

    def incoming(i):
        def values(head):
            return in_v[i, head // 2, :, head % 2 * VDIM : (head % 2 + 1) * VDIM]

        return values, in_l[i].reshape(REQ, TOK)

    falling_l, falling_v = {}, {}
    everything, both = pl.ds(0, TOK), pl.ds(0, 2)

    def settle(rel, awaited, moves):
        def lse_done(lse):
            plse[rel] = lse.reshape(2, REQ // 2, TOK)
            for i, target, span, span_l, peer in moves:
                falling_l[i] = remote(
                    plse.at[rel, span_l], in_l.at[target, span_l], fs.at[i], fr.at[i], peer
                )

        def part_ready(p):
            if awaited is not None:
                falling_v[awaited, p].wait_recv()

        def store(p, at, values):
            pv[rel, p, :, at : at + VDIM] = values

        def part_done(p):
            for i, target, span, span_l, peer in moves:
                falling_v[i, p] = remote(
                    pv.at[rel, p, span], in_v.at[target, p, span], ps.at[i, p], pr.at[i, p], peer
                )

        partials = []
        if awaited is not None:
            falling_l[awaited].wait_recv()
            partials = [incoming(rel)]
        merge(rel, partials, lse_done, part_ready, store, part_done)

    in_v[3, :, half:TOK] = jnp.zeros((QUARTERS, half, VQ), BF16)
    in_v[5, :, 0:half] = jnp.zeros((QUARTERS, half, VQ), BF16)
    in_l[3, 1] = jnp.full((REQ // 2, TOK), LOWEST, F32)
    in_l[5, 0] = jnp.full((REQ // 2, TOK), LOWEST, F32)

    def docs_event(e):
        k, m = e, (e + 2) % CHUNKS
        docs_up[k].wait_recv()
        if e < CHUNKS // 2:
            span = lat(h_down, k * part, part)
            pass_up[e] = remote(span, span, ys.at[0, 5 + e], yr.at[0, 5 + e], up)
        cross(lat(h_down, k * part, part))
        docs_down[m].wait_recv()
        if e < CHUNKS // 2:
            span = lat(h_up, m * part, part)
            pass_down[e] = remote(span, span, ys.at[1, 5 + e], yr.at[1, 5 + e], down)
        cross(lat(h_up, m * part, part))

    forward(0)
    for copy in tables:
        copy.wait_recv()
    passed = [remote(tblb, tblx.at[x], us.at[j], ur.at[j], x_peer[j]) for j in range(1, NX)]
    tblx[pl.ds(x, 1)] = tblb[...].reshape(1, NZ, 1, TBL)
    own_table = here(tblb, sm_own, 6)
    send_docs(2)
    send_docs(3)
    for copy in weights_in:
        copy.wait()
    own_start()
    own_lat.wait()
    for copy in crossed[0:2]:
        copy.wait_recv()
    turn(y)
    advance(1)
    forward(7)
    forward(1)
    for copy in passed:
        copy.wait_recv()
    got_table = here(tblx, sm_got, 7)
    docs_event(0)
    docs_event(1)
    take_in(0)
    advance(2)
    forward(6)
    forward(2)
    rope_up.wait_recv()
    span = rope(h_down, 0, DOC_DEV // 2)
    pass_up[2] = remote(span, span, ys.at[0, 7], yr.at[0, 7], up)
    cross(rope(h_down))
    rope_down.wait_recv()
    span = rope(h_up, DOC_DEV // 2, DOC_DEV // 2)
    pass_down[2] = remote(span, span, ys.at[1, 7], yr.at[1, 7], down)
    cross(rope(h_up))
    take_in(7)
    take_in(1)
    advance(3)
    forward(5)
    forward(3)
    docs_event(2)
    docs_event(3)
    for k in range(CHUNKS):
        hops[k * 2 // CHUNKS, 3, k].wait_recv()
    forward(4)
    take_in(6)
    take_in(2)
    for copy in crossed[2:12]:
        copy.wait_recv()
    turn((y + 1) % NY)
    pass_up[2].wait_recv()
    cross(rope(h_far, 0, DOC_DEV // 2))
    pass_down[2].wait_recv()
    cross(rope(h_far, DOC_DEV // 2, DOC_DEV // 2))
    pass_up[0].wait_recv()
    cross(lat(h_far, 0, part))
    pass_down[0].wait_recv()
    cross(lat(h_far, 2 * part, part))
    turn((y + NY - 1) % NY)
    pass_up[1].wait_recv()
    cross(lat(h_far, part, part))
    pass_down[1].wait_recv()
    cross(lat(h_far, 3 * part, part))
    take_in(5)
    take_in(3)
    own_table.wait()
    got_table.wait()
    for copy in crossed[12:16]:
        copy.wait_recv()
    turn((y + 2) % NY, ((0, part), (2 * part, 3 * part)))
    take_in(4)
    for copy in crossed[16:]:
        copy.wait_recv()
    turn((y + 2) % NY, ((part, 2 * part), (3 * part, 4 * part)))

    attend(4)
    attend(3)
    own_part(range(0, REQ))
    for p in range(HALVES):
        project(OWN, p)
    settle(4, None, [(0, 3, low, pl.ds(0, 1), right), (1, 5, high, pl.ds(1, 1), left)])
    attend(5)
    attend(2)
    settle(3, 0, [(2, 2, everything, both, right)])
    settle(5, 1, [(3, 6, everything, both, left)])
    attend(6)
    attend(1)
    settle(2, 2, [(4, 1, everything, both, right)])
    settle(6, 3, [(5, 7, everything, both, left)])
    attend(7)
    attend(0)
    settle(1, 4, [(6, 0, everything, both, right)])
    settle(7, 5, [(7, 4, everything, both, left)])

    def own_values(head):
        at = head % (HD // HALVES) * VDIM
        return vals[OWN, head // (HD // HALVES), :, :, at : at + VDIM].reshape(TOK, VDIM)

    def last_ready(p):
        falling_v[6, p].wait_recv()
        falling_v[7, p].wait_recv()

    def store(p, at, values):
        first = p * VQ + at
        out_ref[:, first : first + VDIM] = values

    def done(_):
        return None

    falling_l[6].wait_recv()
    falling_l[7].wait_recv()
    merge(
        0, [incoming(0), incoming(4), (own_values, lses[OWN].reshape(REQ, TOK))],
        done, last_ready, store, done,
    )
    for copy in sent:
        copy.wait_send()


def whole(q_nope, q_rope, latent_turned, doc_cache, w_uk, w_uv, doc_slot, doc_blocks, pair_doc, pair_req):
    local = pl.BlockSpec(memory_space=pltpu.VMEM)
    anywhere = pl.BlockSpec(memory_space=pl.ANY)
    scalar = pl.BlockSpec(memory_space=pltpu.SMEM)
    dma = pltpu.SemaphoreType.DMA
    return pl.pallas_call(
        whole_kernel,
        out_shape=jax.ShapeDtypeStruct((TOK, VW), BF16),
        in_specs=[anywhere, anywhere, local, anywhere, anywhere, anywhere] + [scalar] * 4,
        out_specs=local,
        scratch_shapes=[
            pltpu.VMEM((DOC_DEV, NY, 2, 2, POS // 2, RANK), BF16),
            pltpu.VMEM((DOC_DEV, NY, 2, POS // 2, LANES), BF16),
            pltpu.VMEM((DOC_DEV, LATENT, DOC_LEN), BF16),
            pltpu.VMEM((DOC_DEV, 2, POS // 2, LATENT), BF16),
            pltpu.VMEM((HD, NOPE, RANK), BF16),
            pltpu.VMEM((HD, RANK, VDIM), BF16),
            pltpu.VMEM((TOK, LATENT), BF16),
            pltpu.VMEM((NZ, TOK, QW), BF16),
            pltpu.VMEM((NZ, NX, ROWS, QW), BF16),
            pltpu.VMEM((NZ, NX, ROWS, QW), BF16),
            pltpu.VMEM((NZ, 1, TBL), jnp.int32),
            pltpu.VMEM((NZ, 1, TBL), jnp.int32),
            pltpu.VMEM((NX, NZ, 1, TBL), jnp.int32),
            pltpu.SMEM((NZ, 1, TBL), jnp.int32),
            pltpu.SMEM((NX, NZ, 1, TBL), jnp.int32),
            pltpu.VMEM(((NZ + 1) * GROUP, HD, Q_LEN, RANK), BF16),
            pltpu.VMEM(((NZ + 1) * GROUP, HD, Q_LEN, ROPE), BF16),
            pltpu.VMEM((GROUP, HD, Q_LEN, VDIM), F32),
            pltpu.VMEM((NZ + 1, HALVES, NX, ROWS, VW // HALVES), BF16),
            pltpu.VMEM((NZ + 1, NX, CAP, TOK), F32),
            pltpu.VMEM((NZ, HALVES, NX, ROWS, VW // HALVES), BF16),
            pltpu.VMEM((NZ, NX, CAP, TOK), F32),
            pltpu.VMEM((NZ, QUARTERS, TOK, VQ), BF16),
            pltpu.VMEM((NZ, 2, REQ // 2, TOK), F32),
            pltpu.VMEM((NZ, QUARTERS, TOK, VQ), BF16),
            pltpu.VMEM((NZ, 2, REQ // 2, TOK), F32),
            dma((2, 4, CHUNKS)), dma((2, 4, CHUNKS)),
            dma((NZ,)), dma((NZ,)),
            dma((NX,)), dma((NX,)),
            dma((NZ, NX)), dma((NZ, NX)),
            dma((2, 8)), dma((2, 8)),
            dma((18,)), dma((18,)),
            dma((NZ, HALVES, NX)), dma((NZ, HALVES, NX)),
            dma((NZ, NX)), dma((NZ, NX)),
            dma((8, QUARTERS)), dma((8, QUARTERS)),
            dma((8,)), dma((8,)),
            dma((8,)),
        ],
        compiler_params=pltpu.CompilerParams(
            collective_id=0, has_side_effects=True, vmem_limit_bytes=VMEM_LIMIT
        ),
        name="whole",
    )(q_nope, q_rope, latent_turned, doc_cache, w_uk, w_uv, doc_slot, doc_blocks, pair_doc, pair_req)


def on_device(
    q_nope, q_rope, question_latent, doc_cache, w_uk, w_uv, doc_slot, doc_blocks, pair_doc, pair_req
):
    return whole(
        q_nope, q_rope, question_latent.T, doc_cache.reshape(DOC_DEV, 2, POS // 2, LATENT),
        w_uk, w_uv, doc_slot, doc_blocks, pair_doc, pair_req,
    )


def solution(mesh):
    placed = (
        P("doc", "head"),
        P("doc", "head"),
        P("doc", None),
        P("doc", "head", None),
        P("head", None, None),
        P("head", None, None),
        P(),
        P(),
        P("doc"),
        P("doc"),
    )
    return jax.shard_map(
        on_device, mesh=mesh, in_specs=placed, out_specs=P("doc", "head"), check_vma=False
    )
```
